128 devices in a mesh: band: 16 (over z, x), space: 8 (over y, core).
Axes of the slice: x: 4, y: 4, z: 4, core: 2. Of those that a mesh axis runs over, the one named last changes fastest.
Arguments:
- orbitals: bfloat16 [128, 128, 320, 128], P('band', None, 'space'), may hold values from -8.5 to 8.5
- occupations: float32 [128], P('band'), may hold values from 0.07 to 2.5
Outputs:
- potential: float32 [128, 320, 128], P('band', 'space')
The draws below stay inside these ranges and needn't reach their ends.
All inputs are finite; a program needn't handle non-finite values.
Results may differ from the reference program's by a relative error of at most 0.0003.
Values sent between devices are 32-bit elements; how exact they have to be, the bound alone decides.
No kernel may reach another device: no remote copies, remote signals or barrier semaphores. Data moves between devices by JAX's collectives and lax.ppermute only.
A program may use at most 64 MiB of HBM per device.

```python
import math
import jax
import jax.numpy as jnp
from jax import lax

NY = 128
ITERS = 3
BANDS = 128
X = 128
NZ = 320


def draw_orbitals(key, part):
    first = jax.random.fold_in(jax.random.fold_in(key, 11), 0)
    shape = (BANDS, X, NZ, NY)
    position = jnp.arange(X, dtype=jnp.float32) / (X - 1)
    envelope = jnp.sqrt(0.5 + 1.5 * position)[None, :, None, None]
    base = jnp.clip(jax.random.normal(first, shape, jnp.float32), -6.0, 6.0)
    return (base * envelope).astype(jnp.bfloat16)


def draw_occupations(key, part):
    level = jnp.arange(BANDS, dtype=jnp.float32) / BANDS
    fermi = 2.0 / (1.0 + jnp.exp(4.0 * level - 1.5))
    factor = jax.random.uniform(jax.random.fold_in(key, 23), (BANDS,), jnp.float32, 0.7, 1.3)
    return (fermi * factor).astype(jnp.float32)


def setup_inputs(seed: int = 0) -> dict:
    splits = jax.random.split(jax.random.key(seed), 3)
    orbitals = draw_orbitals(jax.random.fold_in(splits[2], 71), 0)
    occupations = draw_occupations(jax.random.fold_in(splits[2], 71), 0)
    return dict(orbitals=orbitals, occupations=occupations)


four_pi = 4.0 * math.pi


def stencil(padded):
    center = padded[2:-2, 2:-2, 2:-2]
    near = padded[3:-1, 2:-2, 2:-2] + padded[1:-3, 2:-2, 2:-2]
    near = near + padded[2:-2, 3:-1, 2:-2] + padded[2:-2, 1:-3, 2:-2]
    near = near + padded[2:-2, 2:-2, 3:-1] + padded[2:-2, 2:-2, 1:-3]
    distant = padded[4:, 2:-2, 2:-2] + padded[:-4, 2:-2, 2:-2]
    distant = distant + padded[2:-2, 4:, 2:-2] + padded[2:-2, :-4, 2:-2]
    distant = distant + padded[2:-2, 2:-2, 4:] + padded[2:-2, 2:-2, :-4]
    return 7.5 * center - (4.0 / 3.0) * near + (1.0 / 12.0) * distant


def reference(orbitals, occupations):
    def accumulate(index, total):
        wave = lax.dynamic_index_in_dim(orbitals, index, 0, keepdims=False).astype(jnp.float32)
        return total + occupations[index] * wave * wave

    start = jnp.zeros(orbitals.shape[1:], jnp.float32)
    density = lax.fori_loop(0, orbitals.shape[0], accumulate, start) / BANDS
    source = four_pi * density
    potential = jnp.zeros_like(source)
    residual, direction = source, source
    norm_now = jnp.sum(residual * residual)
    for step in range(ITERS):
        image = stencil(jnp.pad(direction, 2))
        alpha = norm_now / jnp.sum(direction * image)
        potential = potential + alpha * direction
        residual = residual - alpha * image
        norm_next = jnp.sum(residual * residual)
        direction = residual + (norm_next / norm_now) * direction
        norm_now = norm_next
    return potential
```

```python
import functools
import math

import jax
import jax.numpy as jnp
from jax import lax
from jax.experimental import pallas as pl
from jax.experimental.pallas import tpu as pltpu
from jax.sharding import Mesh
from jax.sharding import PartitionSpec as P


ITERS = 3
REACH = 2 * ITERS
BAND = ("band_0", "band_1")
SPACE = ("space_0", "space_1")
EVERY = BAND + SPACE
SIDE = 4
F32 = jnp.float32


def device(z, x, y, core):
    return ((z * SIDE + x) * SIDE + y) * 2 + core


def moves(target):
    places = [(z, x, y, c) for z in range(SIDE) for x in range(SIDE) for y in range(SIDE) for c in range(2)]
    return [(device(*p), device(*target(*p))) for p in places]


def ring(phase, distance):
    def target(z, x, y, c):
        if (c == 0) == (phase == 0):
            return z, (x + distance) % SIDE, y, c
        return (z + distance) % SIDE, x, y, c

    return moves(target)


def send(value, pairs):
    return lax.ppermute(value, EVERY, pairs)


def density_body(order, occ, orb, out):
    total = None
    for b in range(orb.shape[0]):
        wave = orb[b].astype(F32)
        term = occ[b] * wave * wave
        total = term if total is None else total + term
    out[0] = total


def density_part(orbitals, weights, order, first):
    bands, rows, cols, lanes = orbitals.shape
    deep = rows // 16
    return pl.pallas_call(
        density_body,
        out_shape=jax.ShapeDtypeStruct((SIDE, deep, cols, lanes), F32),
        grid_spec=pltpu.PrefetchScalarGridSpec(
            num_scalar_prefetch=1,
            grid=(SIDE,),
            in_specs=[
                pl.BlockSpec(memory_space=pltpu.SMEM),
                pl.BlockSpec((bands, deep, cols, lanes), lambda g, o: (0, o[first + g], 0, 0)),
            ],
            out_specs=pl.BlockSpec((1, deep, cols, lanes), lambda g, o: (g, 0, 0, 0)),
        ),
        compiler_params=pltpu.CompilerParams(vmem_limit_bytes=16 * 2**20),
        cost_estimate=pl.CostEstimate(flops=0, bytes_accessed=orbitals.size // 2, transcendentals=0),
        name="density",
    )(order, weights, orbitals)


def own_density(orbitals, weights):
    z, x, c = lax.axis_index("band_0"), lax.axis_index("band_1"), lax.axis_index("space_1")
    slot = jnp.arange(16, dtype=jnp.int32)
    first, second = slot // SIDE, slot % SIDE
    to_z = (z + jnp.where(c == 0, second, first)) % SIDE
    to_x = (x + jnp.where(c == 0, first, second)) % SIDE
    order = to_z * SIDE + to_x
    part = [None] * SIDE
    arrived = []
    for k in (2, 1, 3):
        part[k] = density_part(orbitals, weights, order, k * SIDE)
        arrived.append(send(part[k], ring(0, k)))
    mine = density_part(orbitals, weights, order, 0)
    for other in arrived:
        mine = mine + other
    total = mine[0]
    for other in [send(mine[k], ring(1, k)) for k in (2, 1, 3)]:
        total = total + other
    return total


def with_halo(field):
    band = [(i, i + 1) for i in range(15)]
    low = lax.ppermute(field[-REACH:], BAND, band)
    high = lax.ppermute(field[:REACH], BAND, [(b, a) for a, b in band])
    field = jnp.concatenate([low, field, high], 0)
    first = lax.axis_index("space_1") == 0
    left, right = field[:, :REACH], field[:, -REACH:]
    inside = [(i, i ^ 1) for i in range(8)]
    across = [(1, 2), (2, 1), (3, 4), (4, 3), (5, 6), (6, 5)]
    near = lax.ppermute(jnp.where(first, right, left), SPACE, inside)
    far = lax.ppermute(jnp.where(first, left, right), SPACE, across)
    left, right = jnp.where(first, far, near), jnp.where(first, near, far)
    return jnp.concatenate([left, field, right], 1)


def stencil(padded):
    center = padded[2:-2, 2:-2, 2:-2]
    near = padded[3:-1, 2:-2, 2:-2] + padded[1:-3, 2:-2, 2:-2]
    near = near + padded[2:-2, 3:-1, 2:-2] + padded[2:-2, 1:-3, 2:-2]
    near = near + padded[2:-2, 2:-2, 3:-1] + padded[2:-2, 2:-2, 1:-3]
    distant = padded[4:, 2:-2, 2:-2] + padded[:-4, 2:-2, 2:-2]
    distant = distant + padded[2:-2, 4:, 2:-2] + padded[2:-2, :-4, 2:-2]
    distant = distant + padded[2:-2, 2:-2, 4:] + padded[2:-2, 2:-2, :-4]
    return 7.5 * center - 4.0 / 3.0 * near + 1.0 / 12.0 * distant


def weights_of(moments):
    unit = [m / moments[0] * 0.125**k for k, m in enumerate(moments)]

    def inner(a, b, shift):
        terms = [x * y * unit[i + j + shift] for i, x in enumerate(a) for j, y in enumerate(b)]
        return functools.reduce(lambda p, q: p + q, terms)

    residual, direction, answer = [1.0], [1.0], []
    norm = unit[0]
    for step in range(ITERS):
        alpha = norm / inner(direction, direction, 1)
        old = answer + [0.0] * (len(direction) - len(answer))
        answer = [a + alpha * d for a, d in zip(old, direction)]
        if step + 1 < ITERS:
            residual = [r - alpha * d for r, d in zip(residual + [0.0], [0.0] + direction)]
            fresh = inner(residual, residual, 0)
            ratio = fresh / norm
            direction = [r + ratio * d for r, d in zip(residual, direction + [0.0])]
            norm = fresh
    return [a * 0.125 ** (k + 1) for k, a in enumerate(answer)]


def local(orbitals, occupations):
    rows, cols, lanes = orbitals.shape[1] // 16, orbitals.shape[2], orbitals.shape[3]
    scale = 4.0 * math.pi / (orbitals.shape[0] * 16)
    source = own_density(orbitals, occupations * scale)
    wide = with_halo(source)
    band = lax.axis_index(BAND)
    space = lax.axis_index(SPACE)
    row = band * rows - REACH + jnp.arange(wide.shape[0])[:, None, None]
    col = space * cols - REACH + jnp.arange(wide.shape[1])[None, :, None]
    inside = (row >= 0) & (row < 16 * rows) & (col >= 0) & (col < 8 * cols)
    fields = [wide]
    for step in range(ITERS):
        image = stencil(jnp.pad(fields[-1], ((0, 0), (0, 0), (2, 2))))
        edge = 2 * (step + 1)
        fields.append(jnp.where(inside[edge:-edge, edge:-edge], image, 0.0))
    own = []
    for step, field in enumerate(fields):
        edge = REACH - 2 * step
        own.append(field[edge : edge + rows, edge : edge + cols])
    sums = [jnp.sum(own[(k) // 2] * own[(k + 1) // 2]) for k in range(2 * ITERS)]
    lane = jnp.arange(lanes)
    line = functools.reduce(lambda p, q: p + q, [jnp.where(lane == k, m, 0.0) for k, m in enumerate(sums)])
    lines = jnp.broadcast_to(line[None, None], (128, 1, lanes))
    lines = lax.all_to_all(lines, EVERY, split_axis=0, concat_axis=0, tiled=True)
    total = jnp.sum(lines, (0, 1))
    factors = weights_of([total[k] for k in range(2 * ITERS)])
    return factors[0] * own[0] + factors[1] * own[1] + factors[2] * own[2]


def solution(mesh):
    split = Mesh(mesh.devices.reshape(SIDE, SIDE, SIDE, 2), EVERY)
    in_specs = (P(BAND, None, SPACE, None), P(BAND))
    out_specs = P(BAND, SPACE, None)
    return jax.shard_map(local, mesh=split, in_specs=in_specs, out_specs=out_specs, check_vma=False)
```

```python
import functools
import math

import jax
import jax.numpy as jnp
from jax import lax
from jax.experimental import pallas as pl
from jax.experimental.pallas import tpu as pltpu
from jax.sharding import Mesh
from jax.sharding import PartitionSpec as P


ITERS = 3
REACH = 2 * ITERS
BAND = ("band_0", "band_1")
SPACE = ("space_0", "space_1")
EVERY = BAND + SPACE
SIDE = 4
F32 = jnp.float32


def device(z, x, y, core):
    return ((z * SIDE + x) * SIDE + y) * 2 + core


def moves(target):
    places = [(z, x, y, c) for z in range(SIDE) for x in range(SIDE) for y in range(SIDE) for c in range(2)]
    return [(device(*p), device(*target(*p))) for p in places]


def ring(phase, distance):
    def target(z, x, y, c):
        if (c == 0) == (phase == 0):
            return z, (x + distance) % SIDE, y, c
        return (z + distance) % SIDE, x, y, c

    return moves(target)


def send(value, pairs):
    return lax.ppermute(value, EVERY, pairs)


def density_body(order, occ, orb, out):
    total = None
    for b in range(orb.shape[0]):
        wave = orb[b].astype(F32)
        term = occ[b] * wave * wave
        total = term if total is None else total + term
    out[0] = total


def density_part(orbitals, weights, order, first):
    bands, rows, cols, lanes = orbitals.shape
    deep = rows // 16
    return pl.pallas_call(
        density_body,
        out_shape=jax.ShapeDtypeStruct((SIDE, deep, cols, lanes), F32),
        grid_spec=pltpu.PrefetchScalarGridSpec(
            num_scalar_prefetch=1,
            grid=(SIDE,),
            in_specs=[
                pl.BlockSpec(memory_space=pltpu.SMEM),
                pl.BlockSpec((bands, deep, cols, lanes), lambda g, o: (0, o[first + g], 0, 0)),
            ],
            out_specs=pl.BlockSpec((1, deep, cols, lanes), lambda g, o: (g, 0, 0, 0)),
        ),
        compiler_params=pltpu.CompilerParams(vmem_limit_bytes=52 * 2**20),
        cost_estimate=pl.CostEstimate(flops=0, bytes_accessed=orbitals.size // 2, transcendentals=0),
        name="density",
    )(order, weights, orbitals)


def own_density(orbitals, weights):
    z, x, c = lax.axis_index("band_0"), lax.axis_index("band_1"), lax.axis_index("space_1")
    slot = jnp.arange(16, dtype=jnp.int32)
    first, second = slot // SIDE, slot % SIDE
    to_z = (z + jnp.where(c == 0, second, first)) % SIDE
    to_x = (x + jnp.where(c == 0, first, second)) % SIDE
    order = to_z * SIDE + to_x
    part = [None] * SIDE
    arrived = []
    for k in (2, 1, 3):
        part[k] = density_part(orbitals, weights, order, k * SIDE)
        arrived.append(send(part[k], ring(0, k)))
    mine = density_part(orbitals, weights, order, 0)
    for other in arrived:
        mine = mine + other
    total = mine[0]
    for other in [send(mine[k], ring(1, k)) for k in (2, 1, 3)]:
        total = total + other
    return total


def halo(field):
    band = [(i, i + 1) for i in range(15)]
    low = lax.ppermute(field[-REACH:], BAND, band)
    high = lax.ppermute(field[:REACH], BAND, [(b, a) for a, b in band])
    field = jnp.concatenate([low, field, high], 0)
    first = lax.axis_index("space_1") == 0
    left, right = field[:, :REACH], field[:, -REACH:]
    inside = [(i, i ^ 1) for i in range(8)]
    across = [(1, 2), (2, 1), (3, 4), (4, 3), (5, 6), (6, 5)]
    near = lax.ppermute(jnp.where(first, right, left), SPACE, inside)
    far = lax.ppermute(jnp.where(first, left, right), SPACE, across)
    return low, high, near, far


def laplacian(ref, r, lane):
    center = ref[r]
    wide = center.shape[0]

    def across(k):
        return pltpu.roll(center, k % wide, 0)

    def along(k):
        moved = pltpu.roll(center, k % center.shape[1], 1)
        inside = lane >= k if k > 0 else lane < center.shape[1] + k
        return jnp.where(inside, moved, 0.0)

    near = ref[r + 1] + ref[r - 1] + across(-1) + across(1) + along(-1) + along(1)
    distant = ref[r + 2] + ref[r - 2] + across(-2) + across(2) + along(-2) + along(2)
    return 7.5 * center - 4.0 / 3.0 * near + 1.0 / 12.0 * distant


PAD = 8


def krylov_body(place, own, low, high, near, far, first_out, second_out, lines, zero, one, two):
    rows, cols, lanes = own.shape
    deep = rows + 2 * REACH
    band, space, core = place[0], place[1], place[2]
    zero[:, 0:PAD] = jnp.zeros((deep, PAD, lanes), F32)
    zero[:, PAD + cols : 2 * PAD + cols] = jnp.zeros((deep, PAD, lanes), F32)
    zero[0:REACH, PAD : PAD + cols] = low[...]
    zero[REACH : REACH + rows, PAD : PAD + cols] = own[...]
    zero[REACH + rows : deep, PAD : PAD + cols] = high[...]

    @pl.when(core == 0)
    def _():
        zero[:, PAD - REACH : PAD] = far[...]
        zero[:, PAD + cols : PAD + cols + REACH] = near[...]

    @pl.when(core == 1)
    def _():
        zero[:, PAD - REACH : PAD] = near[...]
        zero[:, PAD + cols : PAD + cols + REACH] = far[...]

    shape = (cols + 2 * PAD, lanes)
    lane = lax.broadcasted_iota(jnp.int32, shape, 1)
    col = lax.broadcasted_iota(jnp.int32, shape, 0) + (space * cols - PAD)
    col_in = (col >= 0) & (col < 8 * cols)

    def advance(source, target, edge):
        def step(r, carry):
            row = band * rows + (r - REACH)
            row_in = (row >= 0) & (row < 16 * rows)
            target[r] = jnp.where(col_in & row_in, laplacian(source, r, lane), 0.0)
            return carry

        lax.fori_loop(edge, deep - edge, step, 0)

    advance(zero, one, 2)
    advance(one, two, 4)

    def fold(p, q):
        product = p * q
        return functools.reduce(lambda a, b: a + b, [product[i : i + 8] for i in range(0, cols, 8)])

    def gather(r, sums):
        at = r + REACH
        s0 = zero[at, PAD : PAD + cols]
        s1 = one[at, PAD : PAD + cols]
        s2 = two[at, PAD : PAD + cols]
        s3 = laplacian(two, at, lane)[PAD : PAD + cols]
        first_out[r] = s1
        second_out[r] = s2
        pairs = ((s0, s0), (s0, s1), (s1, s1), (s1, s2), (s2, s2), (s2, s3))
        return tuple(t + fold(p, q) for t, (p, q) in zip(sums, pairs))

    sums = lax.fori_loop(0, rows, gather, tuple(jnp.zeros((8, lanes), F32) for _ in range(2 * ITERS)))
    spot = lax.broadcasted_iota(jnp.int32, (1, lanes), 1)
    line = jnp.zeros((1, lanes), F32)
    for k, part in enumerate(sums):
        whole = jnp.sum(jnp.sum(part, axis=0, keepdims=True), axis=1, keepdims=True)
        line = line + jnp.where(spot == k, whole, 0.0)
    lines[...] = jnp.broadcast_to(line[None], lines.shape)


def krylov(place, own, low, high, near, far):
    rows, cols, lanes = own.shape
    scratch = pltpu.VMEM((rows + 2 * REACH, cols + 2 * PAD, lanes), F32)
    vmem = pl.BlockSpec(memory_space=pltpu.VMEM)
    field = jax.ShapeDtypeStruct(own.shape, F32)
    return pl.pallas_call(
        krylov_body,
        out_shape=(field, field, jax.ShapeDtypeStruct((128, 1, lanes), F32)),
        in_specs=[pl.BlockSpec(memory_space=pltpu.SMEM)] + [vmem] * 5,
        out_specs=(vmem, vmem, vmem),
        scratch_shapes=[scratch, scratch, scratch],
        compiler_params=pltpu.CompilerParams(vmem_limit_bytes=8 * 2**20),
        name="krylov",
    )(place, own, low, high, near, far)


def weights_of(moments):
    unit = [m / moments[0] * 0.125**k for k, m in enumerate(moments)]

    def inner(a, b, shift):
        terms = [x * y * unit[i + j + shift] for i, x in enumerate(a) for j, y in enumerate(b)]
        return functools.reduce(lambda p, q: p + q, terms)

    residual, direction, answer = [1.0], [1.0], []
    norm = unit[0]
    for step in range(ITERS):
        alpha = norm / inner(direction, direction, 1)
        old = answer + [0.0] * (len(direction) - len(answer))
        answer = [a + alpha * d for a, d in zip(old, direction)]
        if step + 1 < ITERS:
            residual = [r - alpha * d for r, d in zip(residual + [0.0], [0.0] + direction)]
            fresh = inner(residual, residual, 0)
            ratio = fresh / norm
            direction = [r + ratio * d for r, d in zip(residual, direction + [0.0])]
            norm = fresh
    return [a * 0.125 ** (k + 1) for k, a in enumerate(answer)]


def combine_body(lines, own, first, second, out):
    line = jnp.sum(lines[...], axis=0)
    spot = lax.broadcasted_iota(jnp.int32, line.shape, 1)
    moments = [jnp.sum(jnp.where(spot == k, line, 0.0), axis=1, keepdims=True) for k in range(2 * ITERS)]
    factors = [jnp.broadcast_to(f, own.shape[1:]) for f in weights_of(moments)]
    for r in range(own.shape[0]):
        out[r] = factors[0] * own[r] + factors[1] * first[r] + factors[2] * second[r]


def combine(lines, own, first, second):
    vmem = pl.BlockSpec(memory_space=pltpu.VMEM)
    return pl.pallas_call(
        combine_body,
        out_shape=jax.ShapeDtypeStruct(own.shape, F32),
        in_specs=[vmem] * 4,
        out_specs=vmem,
        compiler_params=pltpu.CompilerParams(vmem_limit_bytes=8 * 2**20),
        name="combine",
    )(lines, own, first, second)


def local(orbitals, occupations):
    scale = 4.0 * math.pi / (orbitals.shape[0] * 16)
    source = own_density(orbitals, occupations * scale)
    place = jnp.stack([lax.axis_index(BAND), lax.axis_index(SPACE), lax.axis_index("space_1")])
    first, second, lines = krylov(place.astype(jnp.int32), source, *halo(source))
    lines = lax.all_to_all(lines, EVERY, split_axis=0, concat_axis=0, tiled=True)
    return combine(lines, source, first, second)


def solution(mesh):
    split = Mesh(mesh.devices.reshape(SIDE, SIDE, SIDE, 2), EVERY)
    in_specs = (P(BAND, None, SPACE, None), P(BAND))
    out_specs = P(BAND, SPACE, None)
    return jax.shard_map(local, mesh=split, in_specs=in_specs, out_specs=out_specs, check_vma=False)
```

```python
import functools
import math

import jax
import jax.numpy as jnp
from jax import lax
from jax.experimental import pallas as pl
from jax.experimental.pallas import tpu as pltpu
from jax.sharding import Mesh
from jax.sharding import PartitionSpec as P


ITERS = 3
REACH = 2 * ITERS
BAND = ("band_0", "band_1")
SPACE = ("space_0", "space_1")
EVERY = BAND + SPACE
SIDE = 4
F32 = jnp.float32


def device(z, x, y, core):
    return ((z * SIDE + x) * SIDE + y) * 2 + core


def moves(target):
    places = [(z, x, y, c) for z in range(SIDE) for x in range(SIDE) for y in range(SIDE) for c in range(2)]
    return [(device(*p), device(*target(*p))) for p in places]


def partner(phase, k):
    def target(z, x, y, c):
        if (c == 0) == (phase == 0):
            return z, x ^ k, y, c
        return z ^ k, x, y, c

    return moves(target)


def send(value, pairs):
    return lax.ppermute(value, EVERY, pairs)


def density_body(first, scale, orb, occ, out, held, level, arrive, ready):
    z, x, core = lax.axis_index("band_0"), lax.axis_index("band_1"), lax.axis_index("space_1")
    bands, deep = held.shape[1], held.shape[2]
    weights = pltpu.make_async_copy(occ, level, ready)
    weights.start()
    copies = []
    for second in range(SIDE):
        to_z = z ^ jnp.where(core == 0, second, first)
        to_x = x ^ jnp.where(core == 0, first, second)
        row = (to_z * SIDE + to_x) * deep
        copies.append(pltpu.make_async_copy(orb.at[:, pl.ds(row, deep)], held.at[second], arrive.at[second]))
        copies[-1].start()
    weights.wait()
    factor = [level[b] * scale for b in range(bands)]
    for second in range(SIDE):
        copies[second].wait()

        def row(r, carry):
            total = None
            for b in range(bands):
                wave = held[second, b, r].astype(F32)
                term = factor[b] * wave * wave
                total = term if total is None else total + term
            out[second, r] = total
            return carry

        lax.fori_loop(0, deep, row, 0)


def density_part(orbitals, occupations, scale, first):
    bands, rows, cols, lanes = orbitals.shape
    deep = rows // 16
    return pl.pallas_call(
        functools.partial(density_body, first, scale),
        out_shape=jax.ShapeDtypeStruct((SIDE, deep, cols, lanes), F32),
        in_specs=[pl.BlockSpec(memory_space=pl.ANY), pl.BlockSpec(memory_space=pltpu.HBM)],
        out_specs=pl.BlockSpec(memory_space=pltpu.VMEM),
        scratch_shapes=[
            pltpu.VMEM((SIDE, bands, deep, cols, lanes), orbitals.dtype),
            pltpu.SMEM((bands,), F32),
            pltpu.SemaphoreType.DMA((SIDE,)),
            pltpu.SemaphoreType.DMA,
        ],
        compiler_params=pltpu.CompilerParams(vmem_limit_bytes=52 * 2**20),
        cost_estimate=pl.CostEstimate(flops=0, bytes_accessed=orbitals.size // 2, transcendentals=0),
        name="density",
    )(orbitals, occupations)


def own_density(orbitals, occupations, scale):
    part = [None] * SIDE
    arrived = []
    for k in (2, 1, 3):
        part[k] = density_part(orbitals, occupations, scale, k)
        arrived.append(send(part[k], partner(0, k)))
    mine = density_part(orbitals, occupations, scale, 0)
    for other in arrived:
        mine = mine + other
    total = mine[0]
    for other in [send(mine[k], partner(1, k)) for k in (2, 1, 3)]:
        total = total + other
    return total


def across(y, core):
    space = 2 * y + core
    space = space + 1 if core else space - 1
    return (space // 2, space % 2) if 0 <= space < 8 else None


def beside():
    pairs = []
    for z in range(SIDE):
        for x in range(SIDE):
            for y in range(SIDE):
                for c in range(2):
                    if across(y, c) is not None:
                        pairs.append((device(z, x, y, c), device(z, x, *across(y, c))))
    return pairs


def halo(field):
    first = lax.axis_index("space_1") == 0
    left, right = field[:, :REACH], field[:, -REACH:]
    far = send(jnp.where(first, left, right), beside())
    near = lax.ppermute(jnp.where(first, right, left), "space_1", [(0, 1), (1, 0)])
    left, right = jnp.where(first, far, near), jnp.where(first, near, far)
    wide = jnp.concatenate([left, field, right], 1)
    even = lax.axis_index("band_1") % 2 == 0
    inner, outer = [(i, i ^ 1) for i in range(16)], []
    for i in range(1, 15, 2):
        outer += [(i, i + 1), (i + 1, i)]
    first_rows, last_rows = wide[:REACH], wide[-REACH:]
    inner = lax.ppermute(jnp.where(even, last_rows, first_rows), BAND, inner)
    outer = lax.ppermute(jnp.where(even, first_rows, last_rows), BAND, outer)
    return left, right, inner, outer


def laplacian(ref, r, start, size, masks):
    def at(row, shift):
        return ref[row, start + shift : start + shift + size]

    center = at(r, 0)
    lanes = center.shape[1]

    def along(k):
        return jnp.where(masks[k], pltpu.roll(center, -k % lanes, 1), 0.0)

    near = at(r + 1, 0) + at(r - 1, 0) + at(r, 1) + at(r, -1) + along(1) + along(-1)
    distant = at(r + 2, 0) + at(r - 2, 0) + at(r, 2) + at(r, -2) + along(2) + along(-2)
    return 7.5 * center - 4.0 / 3.0 * near + 1.0 / 12.0 * distant


PAD = 8


def krylov_body(own, left, right, inner, outer, first_out, second_out, lines, zero, one, two):
    rows, cols, lanes = own.shape
    deep = rows + 2 * REACH
    band, space = lax.axis_index(BAND), lax.axis_index(SPACE)
    wide = slice(PAD - REACH, PAD + cols + REACH)
    zero[REACH : REACH + rows, PAD : PAD + cols] = own[...]
    zero[REACH : REACH + rows, PAD - REACH : PAD] = left[...]
    zero[REACH : REACH + rows, PAD + cols : PAD + cols + REACH] = right[...]

    @pl.when(band % 2 == 0)
    def _():
        zero[0:REACH, wide] = outer[...]
        zero[REACH + rows : deep, wide] = inner[...]

    @pl.when(band % 2 == 1)
    def _():
        zero[0:REACH, wide] = inner[...]
        zero[REACH + rows : deep, wide] = outer[...]

    def masks(size):
        lane = lax.broadcasted_iota(jnp.int32, (size, lanes), 1)
        return {1: lane < lanes - 1, -1: lane >= 1, 2: lane < lanes - 2, -2: lane >= 2}

    def advance(source, target, edge):
        start = PAD - REACH + edge
        size = cols + 2 * (REACH - edge)
        inside = masks(size)
        col = lax.broadcasted_iota(jnp.int32, (size, lanes), 0) + (space * cols + start - PAD)
        col_in = (col >= 0) & (col < 8 * cols)

        def step(i, carry):
            for j in range(4):
                r = edge + 4 * i + j
                row = band * rows + (r - REACH)
                row_in = (row >= 0) & (row < 16 * rows)
                image = laplacian(source, r, start, size, inside)
                target[r, start : start + size] = jnp.where(col_in & row_in, image, 0.0)
            return carry

        lax.fori_loop(0, (deep - 2 * edge) // 4, step, 0)

    advance(zero, one, 2)
    advance(one, two, 4)
    inside = masks(cols)

    def fold(p, q):
        product = p * q
        return functools.reduce(lambda a, b: a + b, [product[i : i + 8] for i in range(0, cols, 8)])

    def gather(i, sums):
        for j in range(4):
            r = 4 * i + j
            at = r + REACH
            s0 = zero[at, PAD : PAD + cols]
            s1 = one[at, PAD : PAD + cols]
            s2 = two[at, PAD : PAD + cols]
            s3 = laplacian(two, at, PAD, cols, inside)
            first_out[r] = s1
            second_out[r] = s2
            pairs = ((s0, s0), (s0, s1), (s1, s1), (s1, s2), (s2, s2), (s2, s3))
            sums = tuple(t + fold(p, q) for t, (p, q) in zip(sums, pairs))
        return sums

    sums = lax.fori_loop(0, rows // 4, gather, tuple(jnp.zeros((8, lanes), F32) for _ in range(2 * ITERS)))
    spot = lax.broadcasted_iota(jnp.int32, (1, lanes), 1)
    line = jnp.zeros((1, lanes), F32)
    for k, part in enumerate(sums):
        whole = jnp.sum(jnp.sum(part, axis=0, keepdims=True), axis=1, keepdims=True)
        line = line + jnp.where(spot == k, whole, 0.0)
    lines[...] = jnp.broadcast_to(line[None], lines.shape)


def krylov(own, pieces):
    rows, cols, lanes = own.shape
    scratch = pltpu.VMEM((rows + 2 * REACH, cols + 2 * PAD, lanes), F32)
    vmem = pl.BlockSpec(memory_space=pltpu.VMEM)
    field = jax.ShapeDtypeStruct(own.shape, F32)
    return pl.pallas_call(
        krylov_body,
        out_shape=(field, field, jax.ShapeDtypeStruct((128, 1, lanes), F32)),
        in_specs=[vmem] * (1 + len(pieces)),
        out_specs=(vmem, vmem, vmem),
        scratch_shapes=[scratch, scratch, scratch],
        compiler_params=pltpu.CompilerParams(vmem_limit_bytes=8 * 2**20),
        name="krylov",
    )(own, *pieces)


def weights_of(moments):
    unit = [m / moments[0] * 0.125**k for k, m in enumerate(moments)]

    def inner(a, b, shift):
        terms = [x * y * unit[i + j + shift] for i, x in enumerate(a) for j, y in enumerate(b)]
        return functools.reduce(lambda p, q: p + q, terms)

    residual, direction, answer = [1.0], [1.0], []
    norm = unit[0]
    for step in range(ITERS):
        alpha = norm / inner(direction, direction, 1)
        old = answer + [0.0] * (len(direction) - len(answer))
        answer = [a + alpha * d for a, d in zip(old, direction)]
        if step + 1 < ITERS:
            residual = [r - alpha * d for r, d in zip(residual + [0.0], [0.0] + direction)]
            fresh = inner(residual, residual, 0)
            ratio = fresh / norm
            direction = [r + ratio * d for r, d in zip(residual, direction + [0.0])]
            norm = fresh
    return [a * 0.125 ** (k + 1) for k, a in enumerate(answer)]


def combine_body(lines, own, first, second, out):
    line = jnp.sum(lines[...], axis=0)
    spot = lax.broadcasted_iota(jnp.int32, line.shape, 1)
    moments = [jnp.sum(jnp.where(spot == k, line, 0.0), axis=1, keepdims=True) for k in range(2 * ITERS)]
    factors = [jnp.broadcast_to(f, own.shape[1:]) for f in weights_of(moments)]
    for r in range(own.shape[0]):
        out[r] = factors[0] * own[r] + factors[1] * first[r] + factors[2] * second[r]


def combine(lines, own, first, second):
    vmem = pl.BlockSpec(memory_space=pltpu.VMEM)
    return pl.pallas_call(
        combine_body,
        out_shape=jax.ShapeDtypeStruct(own.shape, F32),
        in_specs=[vmem] * 4,
        out_specs=vmem,
        compiler_params=pltpu.CompilerParams(vmem_limit_bytes=8 * 2**20),
        name="combine",
    )(lines, own, first, second)


def local(orbitals, occupations):
    scale = 4.0 * math.pi / (orbitals.shape[0] * 16)
    source = own_density(orbitals, occupations, scale)
    first, second, lines = krylov(source, halo(source))
    lines = lax.all_to_all(lines, EVERY, split_axis=0, concat_axis=0, tiled=True)
    return combine(lines, source, first, second)


def solution(mesh):
    split = Mesh(mesh.devices.reshape(SIDE, SIDE, SIDE, 2), EVERY)
    in_specs = (P(BAND, None, SPACE, None), P(BAND))
    out_specs = P(BAND, SPACE, None)
    return jax.shard_map(local, mesh=split, in_specs=in_specs, out_specs=out_specs, check_vma=False)
```

```python
import functools
import math

import jax
import jax.numpy as jnp
from jax import lax
from jax.experimental import pallas as pl
from jax.experimental.pallas import tpu as pltpu
from jax.sharding import Mesh
from jax.sharding import PartitionSpec as P


ITERS = 3
REACH = 2 * ITERS
BAND = ("band_0", "band_1")
SPACE = ("space_0", "space_1")
EVERY = BAND + SPACE
SIDE = 4
F32 = jnp.float32


def device(z, x, y, core):
    return ((z * SIDE + x) * SIDE + y) * 2 + core


def moves(target):
    places = [(z, x, y, c) for z in range(SIDE) for x in range(SIDE) for y in range(SIDE) for c in range(2)]
    return [(device(*p), device(*target(*p))) for p in places]


def partner(phase, k):
    def target(z, x, y, c):
        if (c == 0) == (phase == 0):
            return z, x ^ k, y, c
        return z ^ k, x, y, c

    return moves(target)


def send(value, pairs):
    return lax.ppermute(value, EVERY, pairs)


def density_body(first, scale, orb, occ, out, held, level, arrive, ready):
    z, x, core = lax.axis_index("band_0"), lax.axis_index("band_1"), lax.axis_index("space_1")
    bands, deep = held.shape[1], held.shape[2]
    weights = pltpu.make_async_copy(occ, level, ready)
    weights.start()
    copies = []
    for second in range(SIDE):
        to_z = z ^ jnp.where(core == 0, second, first)
        to_x = x ^ jnp.where(core == 0, first, second)
        row = (to_z * SIDE + to_x) * deep
        copies.append(pltpu.make_async_copy(orb.at[:, pl.ds(row, deep)], held.at[second], arrive.at[second]))
        copies[-1].start()
    weights.wait()
    factor = [level[b] * scale for b in range(bands)]
    for second in range(SIDE):
        copies[second].wait()

        def row(r, carry):
            total = None
            for b in range(bands):
                wave = held[second, b, r].astype(F32)
                term = factor[b] * wave * wave
                total = term if total is None else total + term
            out[second, r] = total
            return carry

        lax.fori_loop(0, deep, row, 0)


def density_part(orbitals, occupations, scale, first):
    bands, rows, cols, lanes = orbitals.shape
    deep = rows // 16
    return pl.pallas_call(
        functools.partial(density_body, first, scale),
        out_shape=jax.ShapeDtypeStruct((SIDE, deep, cols, lanes), F32),
        in_specs=[pl.BlockSpec(memory_space=pl.ANY), pl.BlockSpec(memory_space=pltpu.HBM)],
        out_specs=pl.BlockSpec(memory_space=pltpu.VMEM),
        scratch_shapes=[
            pltpu.VMEM((SIDE, bands, deep, cols, lanes), orbitals.dtype),
            pltpu.SMEM((bands,), F32),
            pltpu.SemaphoreType.DMA((SIDE,)),
            pltpu.SemaphoreType.DMA,
        ],
        compiler_params=pltpu.CompilerParams(vmem_limit_bytes=52 * 2**20),
        cost_estimate=pl.CostEstimate(flops=0, bytes_accessed=orbitals.size // 2, transcendentals=0),
        name="density",
    )(orbitals, occupations)


def own_density(orbitals, occupations, scale):
    part = [None] * SIDE
    arrived = []
    for k in (2, 1, 3):
        part[k] = density_part(orbitals, occupations, scale, k)
        arrived.append(send(part[k], partner(0, k)))
    mine = density_part(orbitals, occupations, scale, 0)
    for other in arrived:
        mine = mine + other
    total = mine[0]
    for other in [send(mine[k], partner(1, k)) for k in (2, 1, 3)]:
        total = total + other
    return total


def across(y, core):
    space = 2 * y + core
    space = (space + 1 if core else space - 1) % 8
    return space // 2, space % 2


def beside():
    pairs = []
    for z in range(SIDE):
        for x in range(SIDE):
            for y in range(SIDE):
                for c in range(2):
                    pairs.append((device(z, x, y, c), device(z, x, *across(y, c))))
    return pairs


def halo(field):
    first = lax.axis_index("space_1") == 0
    left, right = field[:, :REACH], field[:, -REACH:]
    far = send(jnp.where(first, left, right), beside())
    near = lax.ppermute(jnp.where(first, right, left), "space_1", [(0, 1), (1, 0)])
    space = lax.axis_index(SPACE)
    far = jnp.where((space > 0) & (space < 7), far, 0.0)
    left, right = jnp.where(first, far, near), jnp.where(first, near, far)
    wide = jnp.concatenate([left, field, right], 1)
    even = lax.axis_index("band_1") % 2 == 0
    inner = [(i, i ^ 1) for i in range(16)]
    outer = [(i, (i + 1 if i % 2 else i - 1) % 16) for i in range(16)]
    first_rows, last_rows = wide[:REACH], wide[-REACH:]
    inner = lax.ppermute(jnp.where(even, last_rows, first_rows), BAND, inner)
    outer = lax.ppermute(jnp.where(even, first_rows, last_rows), BAND, outer)
    return left, right, inner, outer


def laplacian(ref, r, start, size, masks):
    def at(row, shift):
        return ref[row, start + shift : start + shift + size]

    center = at(r, 0)
    lanes = center.shape[1]

    def along(k):
        return jnp.where(masks[k], pltpu.roll(center, -k % lanes, 1), 0.0)

    near = at(r + 1, 0) + at(r - 1, 0) + at(r, 1) + at(r, -1) + along(1) + along(-1)
    distant = at(r + 2, 0) + at(r - 2, 0) + at(r, 2) + at(r, -2) + along(2) + along(-2)
    return 7.5 * center - 4.0 / 3.0 * near + 1.0 / 12.0 * distant


PAD = 8


def krylov_body(own, left, right, inner, outer, first_out, second_out, lines, zero, one, two):
    rows, cols, lanes = own.shape
    deep = rows + 2 * REACH
    band, space = lax.axis_index(BAND), lax.axis_index(SPACE)
    wide = slice(PAD - REACH, PAD + cols + REACH)
    zero[REACH : REACH + rows, PAD : PAD + cols] = own[...]
    zero[REACH : REACH + rows, PAD - REACH : PAD] = left[...]
    zero[REACH : REACH + rows, PAD + cols : PAD + cols + REACH] = right[...]

    @pl.when(band % 2 == 0)
    def _():
        zero[0:REACH, wide] = jnp.where(band > 0, outer[...], 0.0)
        zero[REACH + rows : deep, wide] = inner[...]

    @pl.when(band % 2 == 1)
    def _():
        zero[0:REACH, wide] = inner[...]
        zero[REACH + rows : deep, wide] = jnp.where(band < 15, outer[...], 0.0)

    def masks(size):
        lane = lax.broadcasted_iota(jnp.int32, (size, lanes), 1)
        return {1: lane < lanes - 1, -1: lane >= 1, 2: lane < lanes - 2, -2: lane >= 2}

    def advance(source, target, edge):
        start = PAD - REACH + edge
        size = cols + 2 * (REACH - edge)
        inside = masks(size)
        col = lax.broadcasted_iota(jnp.int32, (size, lanes), 0) + (space * cols + start - PAD)
        col_in = (col >= 0) & (col < 8 * cols)

        def step(i, carry):
            for j in range(4):
                r = edge + 4 * i + j
                row = band * rows + (r - REACH)
                row_in = (row >= 0) & (row < 16 * rows)
                image = laplacian(source, r, start, size, inside)
                target[r, start : start + size] = jnp.where(col_in & row_in, image, 0.0)
            return carry

        lax.fori_loop(0, (deep - 2 * edge) // 4, step, 0)

    advance(zero, one, 2)
    advance(one, two, 4)
    inside = masks(cols)

    def fold(p, q):
        product = p * q
        return functools.reduce(lambda a, b: a + b, [product[i : i + 8] for i in range(0, cols, 8)])

    def gather(i, sums):
        for j in range(4):
            r = 4 * i + j
            at = r + REACH
            s0 = zero[at, PAD : PAD + cols]
            s1 = one[at, PAD : PAD + cols]
            s2 = two[at, PAD : PAD + cols]
            s3 = laplacian(two, at, PAD, cols, inside)
            first_out[r] = s1
            second_out[r] = s2
            pairs = ((s0, s0), (s0, s1), (s1, s1), (s1, s2), (s2, s2), (s2, s3))
            sums = tuple(t + fold(p, q) for t, (p, q) in zip(sums, pairs))
        return sums

    sums = lax.fori_loop(0, rows // 4, gather, tuple(jnp.zeros((8, lanes), F32) for _ in range(2 * ITERS)))
    spot = lax.broadcasted_iota(jnp.int32, (1, lanes), 1)
    line = jnp.zeros((1, lanes), F32)
    for k, part in enumerate(sums):
        whole = jnp.sum(jnp.sum(part, axis=0, keepdims=True), axis=1, keepdims=True)
        line = line + jnp.where(spot == k, whole, 0.0)
    lines[...] = jnp.broadcast_to(line, lines.shape)


def krylov(own, pieces):
    rows, cols, lanes = own.shape
    scratch = pltpu.VMEM((rows + 2 * REACH, cols + 2 * PAD, lanes), F32)
    vmem = pl.BlockSpec(memory_space=pltpu.VMEM)
    field = jax.ShapeDtypeStruct(own.shape, F32)
    return pl.pallas_call(
        krylov_body,
        out_shape=(field, field, jax.ShapeDtypeStruct((128, lanes), F32)),
        in_specs=[vmem] * (1 + len(pieces)),
        out_specs=(vmem, vmem, vmem),
        scratch_shapes=[scratch, scratch, scratch],
        compiler_params=pltpu.CompilerParams(vmem_limit_bytes=8 * 2**20),
        name="krylov",
    )(own, *pieces)


def weights_of(moments):
    unit = [m / moments[0] * 0.125**k for k, m in enumerate(moments)]

    def inner(a, b, shift):
        terms = [x * y * unit[i + j + shift] for i, x in enumerate(a) for j, y in enumerate(b)]
        return functools.reduce(lambda p, q: p + q, terms)

    residual, direction, answer = [1.0], [1.0], []
    norm = unit[0]
    for step in range(ITERS):
        alpha = norm / inner(direction, direction, 1)
        old = answer + [0.0] * (len(direction) - len(answer))
        answer = [a + alpha * d for a, d in zip(old, direction)]
        if step + 1 < ITERS:
            residual = [r - alpha * d for r, d in zip(residual + [0.0], [0.0] + direction)]
            fresh = inner(residual, residual, 0)
            ratio = fresh / norm
            direction = [r + ratio * d for r, d in zip(residual, direction + [0.0])]
            norm = fresh
    return [a * 0.125 ** (k + 1) for k, a in enumerate(answer)]


def combine_body(lines, own, first, second, out):
    line = jnp.sum(lines[...], axis=0, keepdims=True)
    spot = lax.broadcasted_iota(jnp.int32, line.shape, 1)
    moments = [jnp.sum(jnp.where(spot == k, line, 0.0), axis=1, keepdims=True) for k in range(2 * ITERS)]
    factors = [jnp.broadcast_to(f, own.shape[1:]) for f in weights_of(moments)]
    for r in range(own.shape[0]):
        out[r] = factors[0] * own[r] + factors[1] * first[r] + factors[2] * second[r]


def combine(lines, own, first, second):
    vmem = pl.BlockSpec(memory_space=pltpu.VMEM)
    return pl.pallas_call(
        combine_body,
        out_shape=jax.ShapeDtypeStruct(own.shape, F32),
        in_specs=[vmem] * 4,
        out_specs=vmem,
        compiler_params=pltpu.CompilerParams(vmem_limit_bytes=8 * 2**20),
        name="combine",
    )(lines, own, first, second)


def local(orbitals, occupations):
    scale = 4.0 * math.pi / (orbitals.shape[0] * 16)
    source = own_density(orbitals, occupations, scale)
    first, second, lines = krylov(source, halo(source))
    lines = lax.all_to_all(lines[:, None], EVERY, split_axis=0, concat_axis=0, tiled=True)[:, 0]
    return combine(lines, source, first, second)


def solution(mesh):
    split = Mesh(mesh.devices.reshape(SIDE, SIDE, SIDE, 2), EVERY)
    in_specs = (P(BAND, None, SPACE, None), P(BAND))
    out_specs = P(BAND, SPACE, None)
    return jax.shard_map(local, mesh=split, in_specs=in_specs, out_specs=out_specs, check_vma=False)
```

```python
import functools
import math

import jax
import jax.numpy as jnp
from jax import lax
from jax.experimental import pallas as pl
from jax.experimental.pallas import tpu as pltpu
from jax.sharding import Mesh
from jax.sharding import PartitionSpec as P


ITERS = 3
REACH = 2 * ITERS
BAND = ("band_0", "band_1")
SPACE = ("space_0", "space_1")
EVERY = BAND + SPACE
SIDE = 4
F32 = jnp.float32


def device(z, x, y, core):
    return ((z * SIDE + x) * SIDE + y) * 2 + core


def moves(target):
    places = [(z, x, y, c) for z in range(SIDE) for x in range(SIDE) for y in range(SIDE) for c in range(2)]
    return [(device(*p), device(*target(*p))) for p in places]


def partner(phase, k):
    def target(z, x, y, c):
        if (c == 0) == (phase == 0):
            return z, x ^ k, y, c
        return z ^ k, x, y, c

    return moves(target)


def send(value, pairs):
    return lax.ppermute(value, EVERY, pairs)


CHUNK = 160


def density_body(firsts, scale, orb, occ, *refs):
    outs, (held, level, arrive, ready) = refs[:-4], refs[-4:]
    z, x, core = lax.axis_index("band_0"), lax.axis_index("band_1"), lax.axis_index("space_1")
    bands, deep = held.shape[1:3]
    weights = pltpu.make_async_copy(occ, level, ready)
    copies = []
    for slot in range(len(firsts) * SIDE):
        first, second = firsts[slot // SIDE], slot % SIDE
        to_z = z ^ jnp.where(core == 0, second, first)
        to_x = x ^ jnp.where(core == 0, first, second)
        row = pl.multiple_of((to_z * SIDE + to_x) * deep, deep)
        copies.append(pltpu.make_async_copy(orb.at[:, pl.ds(row, deep)], held.at[slot], arrive.at[slot]))
        copies[-1].start()
        if slot == 0:
            weights.start()
    weights.wait()
    factor = [level[b] * scale for b in range(bands)]
    for slot, copy in enumerate(copies):
        copy.wait()
        out, at = outs[slot // 2], slot % 2

        def part(i, carry):
            rows = pl.ds(pl.multiple_of(i * CHUNK, CHUNK), CHUNK)
            total = None
            for b in range(bands):
                wave = held[slot, b, rows].astype(F32)
                term = factor[b] * wave * wave
                total = term if total is None else total + term
            out[at, rows] = total
            return carry

        lax.fori_loop(0, deep // CHUNK, part, 0)


def density_part(orbitals, occupations, scale, firsts):
    bands, rows, cols, lanes = orbitals.shape
    deep = rows // 16
    slots = len(firsts) * SIDE
    half = jax.ShapeDtypeStruct((SIDE // 2, deep * cols, lanes), F32)
    vmem = pl.BlockSpec(memory_space=pltpu.VMEM)
    hbm = pl.BlockSpec(memory_space=pl.ANY)
    parts = pl.pallas_call(
        functools.partial(density_body, firsts, scale),
        out_shape=(half,) * (2 * len(firsts)),
        in_specs=[hbm, hbm],
        out_specs=(vmem,) * (2 * len(firsts)),
        scratch_shapes=[
            pltpu.VMEM((slots, bands, deep * cols, lanes), orbitals.dtype),
            pltpu.SMEM((bands,), F32),
            pltpu.SemaphoreType.DMA((slots,)),
            pltpu.SemaphoreType.DMA,
        ],
        compiler_params=pltpu.CompilerParams(vmem_limit_bytes=52 * 2**20),
        cost_estimate=pl.CostEstimate(flops=0, bytes_accessed=orbitals.size // 2, transcendentals=0),
        name="density",
    )(orbitals.reshape(bands, rows * cols, lanes), occupations)
    return [p.reshape(SIDE // 2, deep, cols, lanes) for p in parts]


def own_density(orbitals, occupations, scale):
    a2, b2 = density_part(orbitals, occupations, scale, (2,))
    a_near, b_near = send(a2, partner(0, 1)), send(b2, partner(0, 3))
    a1, b1, a3, b3 = density_part(orbitals, occupations, scale, (1, 3))
    a_first, b_first = send(a1, partner(0, 1)), send(b3, partner(0, 3))
    a_near, b_near = lax.optimization_barrier((a_near, b_near))
    b1, a3 = b1 + b_near, a3 + a_near
    b1, a3, late = lax.optimization_barrier((b1, a3, occupations))
    b_last, a_last = send(b1, partner(0, 1)), send(a3, partner(0, 3))
    a0, b0 = density_part(orbitals, late, scale, (0,))
    a_first, a_last, b_first, b_last = lax.optimization_barrier((a_first, a_last, b_first, b_last))
    a0, b0 = a0 + a_first + a_last, b0 + b_first + b_last
    total = a0[0]
    for block, k in ((b0[0], 2), (a0[1], 1), (b0[1], 3)):
        total = total + send(block, partner(1, k))
    return total


def across(y, core):
    space = 2 * y + core
    space = (space + 1 if core else space - 1) % 8
    return space // 2, space % 2


def beside():
    pairs = []
    for z in range(SIDE):
        for x in range(SIDE):
            for y in range(SIDE):
                for c in range(2):
                    pairs.append((device(z, x, y, c), device(z, x, *across(y, c))))
    return pairs


def halo(field):
    first = lax.axis_index("space_1") == 0
    left, right = field[:, :REACH], field[:, -REACH:]
    far = send(jnp.where(first, left, right), beside())
    near = lax.ppermute(jnp.where(first, right, left), "space_1", [(0, 1), (1, 0)])
    space = lax.axis_index(SPACE)
    far = jnp.where((space > 0) & (space < 7), far, 0.0)
    left, right = jnp.where(first, far, near), jnp.where(first, near, far)
    wide = jnp.concatenate([left, field, right], 1)
    even = lax.axis_index("band_1") % 2 == 0
    inner = [(i, i ^ 1) for i in range(16)]
    outer = [(i, (i + 1 if i % 2 else i - 1) % 16) for i in range(16)]
    first_rows, last_rows = wide[:REACH], wide[-REACH:]
    inner = lax.ppermute(jnp.where(even, last_rows, first_rows), BAND, inner)
    outer = lax.ppermute(jnp.where(even, first_rows, last_rows), BAND, outer)
    return left, right, inner, outer


def laplacian(ref, r, start, size, masks):
    def at(row, shift):
        return ref[row, start + shift : start + shift + size]

    center = at(r, 0)
    lanes = center.shape[1]

    def along(k):
        return jnp.where(masks[k], pltpu.roll(center, -k % lanes, 1), 0.0)

    near = at(r + 1, 0) + at(r - 1, 0) + at(r, 1) + at(r, -1) + along(1) + along(-1)
    distant = at(r + 2, 0) + at(r - 2, 0) + at(r, 2) + at(r, -2) + along(2) + along(-2)
    return 7.5 * center - 4.0 / 3.0 * near + 1.0 / 12.0 * distant


PAD = 8


def krylov_body(own, left, right, inner, outer, first_out, second_out, lines, zero, one, two):
    rows, cols, lanes = own.shape
    deep = rows + 2 * REACH
    band, space = lax.axis_index(BAND), lax.axis_index(SPACE)
    wide = slice(PAD - REACH, PAD + cols + REACH)
    zero[REACH : REACH + rows, PAD : PAD + cols] = own[...]
    zero[REACH : REACH + rows, PAD - REACH : PAD] = left[...]
    zero[REACH : REACH + rows, PAD + cols : PAD + cols + REACH] = right[...]

    @pl.when(band % 2 == 0)
    def _():
        zero[0:REACH, wide] = jnp.where(band > 0, outer[...], 0.0)
        zero[REACH + rows : deep, wide] = inner[...]

    @pl.when(band % 2 == 1)
    def _():
        zero[0:REACH, wide] = inner[...]
        zero[REACH + rows : deep, wide] = jnp.where(band < 15, outer[...], 0.0)

    def masks(size):
        lane = lax.broadcasted_iota(jnp.int32, (size, lanes), 1)
        return {1: lane < lanes - 1, -1: lane >= 1, 2: lane < lanes - 2, -2: lane >= 2}

    def advance(source, target, edge):
        start = PAD - REACH + edge
        size = cols + 2 * (REACH - edge)
        inside = masks(size)
        col = lax.broadcasted_iota(jnp.int32, (size, lanes), 0) + (space * cols + start - PAD)
        col_in = (col >= 0) & (col < 8 * cols)

        def step(i, carry):
            for j in range(4):
                r = edge + 4 * i + j
                row = band * rows + (r - REACH)
                row_in = (row >= 0) & (row < 16 * rows)
                image = laplacian(source, r, start, size, inside)
                target[r, start : start + size] = jnp.where(col_in & row_in, image, 0.0)
            return carry

        lax.fori_loop(0, (deep - 2 * edge) // 4, step, 0)

    advance(zero, one, 2)
    advance(one, two, 4)
    inside = masks(cols)

    def fold(p, q):
        product = p * q
        return functools.reduce(lambda a, b: a + b, [product[i : i + 8] for i in range(0, cols, 8)])

    def gather(i, sums):
        for j in range(4):
            r = 4 * i + j
            at = r + REACH
            s0 = zero[at, PAD : PAD + cols]
            s1 = one[at, PAD : PAD + cols]
            s2 = two[at, PAD : PAD + cols]
            s3 = laplacian(two, at, PAD, cols, inside)
            first_out[r] = s1
            second_out[r] = s2
            pairs = ((s0, s0), (s0, s1), (s1, s1), (s1, s2), (s2, s2), (s2, s3))
            sums = tuple(t + fold(p, q) for t, (p, q) in zip(sums, pairs))
        return sums

    sums = lax.fori_loop(0, rows // 4, gather, tuple(jnp.zeros((8, lanes), F32) for _ in range(2 * ITERS)))
    spot = lax.broadcasted_iota(jnp.int32, (1, lanes), 1)
    line = jnp.zeros((1, lanes), F32)
    for k, part in enumerate(sums):
        whole = jnp.sum(jnp.sum(part, axis=0, keepdims=True), axis=1, keepdims=True)
        line = line + jnp.where(spot == k, whole, 0.0)
    lines[...] = jnp.broadcast_to(line, lines.shape)


def krylov(own, pieces):
    rows, cols, lanes = own.shape
    scratch = pltpu.VMEM((rows + 2 * REACH, cols + 2 * PAD, lanes), F32)
    vmem = pl.BlockSpec(memory_space=pltpu.VMEM)
    field = jax.ShapeDtypeStruct(own.shape, F32)
    return pl.pallas_call(
        krylov_body,
        out_shape=(field, field, jax.ShapeDtypeStruct((128, lanes), F32)),
        in_specs=[vmem] * (1 + len(pieces)),
        out_specs=(vmem, vmem, vmem),
        scratch_shapes=[scratch, scratch, scratch],
        compiler_params=pltpu.CompilerParams(vmem_limit_bytes=8 * 2**20),
        name="krylov",
    )(own, *pieces)


def weights_of(moments):
    unit = [m / moments[0] * 0.125**k for k, m in enumerate(moments)]

    def inner(a, b, shift):
        terms = [x * y * unit[i + j + shift] for i, x in enumerate(a) for j, y in enumerate(b)]
        return functools.reduce(lambda p, q: p + q, terms)

    residual, direction, answer = [1.0], [1.0], []
    norm = unit[0]
    for step in range(ITERS):
        alpha = norm / inner(direction, direction, 1)
        old = answer + [0.0] * (len(direction) - len(answer))
        answer = [a + alpha * d for a, d in zip(old, direction)]
        if step + 1 < ITERS:
            residual = [r - alpha * d for r, d in zip(residual + [0.0], [0.0] + direction)]
            fresh = inner(residual, residual, 0)
            ratio = fresh / norm
            direction = [r + ratio * d for r, d in zip(residual, direction + [0.0])]
            norm = fresh
    return [a * 0.125 ** (k + 1) for k, a in enumerate(answer)]


def combine_body(lines, own, first, second, out):
    line = jnp.sum(lines[...], axis=0, keepdims=True)
    spot = lax.broadcasted_iota(jnp.int32, line.shape, 1)
    moments = [jnp.sum(jnp.where(spot == k, line, 0.0), axis=1, keepdims=True) for k in range(2 * ITERS)]
    factors = [jnp.broadcast_to(f, own.shape[1:]) for f in weights_of(moments)]
    for r in range(own.shape[0]):
        out[r] = factors[0] * own[r] + factors[1] * first[r] + factors[2] * second[r]


def combine(lines, own, first, second):
    vmem = pl.BlockSpec(memory_space=pltpu.VMEM)
    return pl.pallas_call(
        combine_body,
        out_shape=jax.ShapeDtypeStruct(own.shape, F32),
        in_specs=[vmem] * 4,
        out_specs=vmem,
        compiler_params=pltpu.CompilerParams(vmem_limit_bytes=8 * 2**20),
        name="combine",
    )(lines, own, first, second)


def local(orbitals, occupations):
    scale = 4.0 * math.pi / (orbitals.shape[0] * 16)
    source = own_density(orbitals, occupations, scale)
    first, second, lines = krylov(source, halo(source))
    lines = lax.all_to_all(lines[:, None], EVERY, split_axis=0, concat_axis=0, tiled=True)[:, 0]
    return combine(lines, source, first, second)


def solution(mesh):
    split = Mesh(mesh.devices.reshape(SIDE, SIDE, SIDE, 2), EVERY)
    in_specs = (P(BAND, None, SPACE, None), P(BAND))
    out_specs = P(BAND, SPACE, None)
    return jax.shard_map(local, mesh=split, in_specs=in_specs, out_specs=out_specs, check_vma=False)
```

```python
import functools
import math

import jax
import jax.numpy as jnp
from jax import lax
from jax.experimental import pallas as pl
from jax.experimental.pallas import tpu as pltpu
from jax.sharding import Mesh
from jax.sharding import PartitionSpec as P


ITERS = 3
REACH = 2 * ITERS - 1
SIDEWAYS = REACH - 1
BAND = ("band_0", "band_1")
SPACE = ("space_0", "space_1")
EVERY = BAND + SPACE
SIDE = 4
F32 = jnp.float32


def device(z, x, y, core):
    return ((z * SIDE + x) * SIDE + y) * 2 + core


def moves(target):
    places = [(z, x, y, c) for z in range(SIDE) for x in range(SIDE) for y in range(SIDE) for c in range(2)]
    return [(device(*p), device(*target(*p))) for p in places]


def partner(phase, k):
    def target(z, x, y, c):
        if (c == 0) == (phase == 0):
            return z, x ^ k, y, c
        return z ^ k, x, y, c

    return moves(target)


def send(value, pairs):
    return lax.ppermute(value, EVERY, pairs)


CHUNK = 160


def density_body(firsts, scale, orb, occ, *refs):
    outs, (held, level, arrive, ready) = refs[:-4], refs[-4:]
    z, x, core = lax.axis_index("band_0"), lax.axis_index("band_1"), lax.axis_index("space_1")
    bands, deep = held.shape[1:3]
    weights = pltpu.make_async_copy(occ, level, ready)
    copies = []
    for slot in range(len(firsts) * SIDE):
        first, second = firsts[slot // SIDE], slot % SIDE
        to_z = z ^ jnp.where(core == 0, second, first)
        to_x = x ^ jnp.where(core == 0, first, second)
        row = pl.multiple_of((to_z * SIDE + to_x) * deep, deep)
        copies.append(pltpu.make_async_copy(orb.at[:, pl.ds(row, deep)], held.at[slot], arrive.at[slot]))
        copies[-1].start()
        if slot == 0:
            weights.start()
    weights.wait()
    factor = [level[b] * scale for b in range(bands)]
    for slot, copy in enumerate(copies):
        copy.wait()
        out, at = outs[slot // 2], slot % 2

        def part(i, carry):
            rows = pl.ds(pl.multiple_of(i * CHUNK, CHUNK), CHUNK)
            total = None
            for b in range(bands):
                wave = held[slot, b, rows].astype(F32)
                term = factor[b] * wave * wave
                total = term if total is None else total + term
            out[at, rows] = total
            return carry

        lax.fori_loop(0, deep // CHUNK, part, 0)


def density_part(orbitals, occupations, scale, firsts):
    bands, rows, cols, lanes = orbitals.shape
    deep = rows // 16
    slots = len(firsts) * SIDE
    half = jax.ShapeDtypeStruct((SIDE // 2, deep * cols, lanes), F32)
    vmem = pl.BlockSpec(memory_space=pltpu.VMEM)
    hbm = pl.BlockSpec(memory_space=pl.ANY)
    parts = pl.pallas_call(
        functools.partial(density_body, firsts, scale),
        out_shape=(half,) * (2 * len(firsts)),
        in_specs=[hbm, hbm],
        out_specs=(vmem,) * (2 * len(firsts)),
        scratch_shapes=[
            pltpu.VMEM((slots, bands, deep * cols, lanes), orbitals.dtype),
            pltpu.SMEM((bands,), F32),
            pltpu.SemaphoreType.DMA((slots,)),
            pltpu.SemaphoreType.DMA,
        ],
        compiler_params=pltpu.CompilerParams(vmem_limit_bytes=52 * 2**20),
        cost_estimate=pl.CostEstimate(flops=0, bytes_accessed=orbitals.size // 2, transcendentals=0),
        name="density",
    )(orbitals.reshape(bands, rows * cols, lanes), occupations)
    return [p.reshape(SIDE // 2, deep, cols, lanes) for p in parts]


def own_density(orbitals, occupations, scale):
    a2, b2 = density_part(orbitals, occupations, scale, (2,))
    a_near, b_near = send(a2, partner(0, 1)), send(b2, partner(0, 3))
    a1, b1, a3, b3 = density_part(orbitals, occupations, scale, (1, 3))
    a_first, b_first = send(a1, partner(0, 1)), send(b3, partner(0, 3))
    a_near, b_near = lax.optimization_barrier((a_near, b_near))
    b1, a3 = b1 + b_near, a3 + a_near
    b1, a3, late = lax.optimization_barrier((b1, a3, occupations))
    b_last, a_last = send(b1, partner(0, 1)), send(a3, partner(0, 3))
    a0, b0 = density_part(orbitals, late, scale, (0,))
    a_first, a_last, b_first, b_last = lax.optimization_barrier((a_first, a_last, b_first, b_last))
    a0, b0 = a0 + a_first + a_last, b0 + b_first + b_last
    total = a0[0]
    for block, k in ((b0[0], 2), (a0[1], 1), (b0[1], 3)):
        total = total + send(block, partner(1, k))
    return total


def across(y, core):
    space = 2 * y + core
    space = (space + 1 if core else space - 1) % 8
    return space // 2, space % 2


def beside():
    pairs = []
    for z in range(SIDE):
        for x in range(SIDE):
            for y in range(SIDE):
                for c in range(2):
                    pairs.append((device(z, x, y, c), device(z, x, *across(y, c))))
    return pairs


def halo(field):
    first = lax.axis_index("space_1") == 0
    left, right = field[:, :REACH], field[:, -REACH:]
    far = send(jnp.where(first, left, right), beside())
    near = lax.ppermute(jnp.where(first, right, left), "space_1", [(0, 1), (1, 0)])
    space = lax.axis_index(SPACE)
    far = jnp.where((space > 0) & (space < 7), far, 0.0)
    left, right = jnp.where(first, far, near), jnp.where(first, near, far)
    wide = jnp.concatenate([left[:, -SIDEWAYS:], field, right[:, :SIDEWAYS]], 1)
    even = lax.axis_index("band_1") % 2 == 0
    inner = [(i, i ^ 1) for i in range(16)]
    outer = [(i, (i + 1 if i % 2 else i - 1) % 16) for i in range(16)]
    first_rows, last_rows = wide[:REACH], wide[-REACH:]
    inner = lax.ppermute(jnp.where(even, last_rows, first_rows), BAND, inner)
    outer = lax.ppermute(jnp.where(even, first_rows, last_rows), BAND, outer)
    return left, right, inner, outer


def laplacian(ref, r, start, size, masks, outer=None):
    outer = ref if outer is None else outer

    def at(down, across):
        source = outer if abs(down) + abs(across) == 2 else ref
        return source[r + down, start + across : start + across + size]

    center = at(0, 0)
    lanes = center.shape[1]

    def along(k):
        return jnp.where(masks[k], pltpu.roll(center, -k % lanes, 1), 0.0)

    near = at(1, 0) + at(-1, 0) + at(0, 1) + at(0, -1) + along(1) + along(-1)
    distant = at(2, 0) + at(-2, 0) + at(0, 2) + at(0, -2) + along(2) + along(-2)
    return 7.5 * center - 4.0 / 3.0 * near + 1.0 / 12.0 * distant


PAD = 8


def krylov_body(own, left, right, inner, outer, first_out, second_out, lines, zero, one, two, double):
    rows, cols, lanes = own.shape
    deep = rows + 2 * REACH
    band, space = lax.axis_index(BAND), lax.axis_index(SPACE)
    wide = slice(PAD - SIDEWAYS, PAD + cols + SIDEWAYS)
    for edge in (slice(0, REACH), slice(REACH + rows, deep)):
        zero[edge, 0:PAD] = jnp.zeros((REACH, PAD, lanes), F32)
        zero[edge, PAD + cols :] = jnp.zeros((REACH, PAD, lanes), F32)
    zero[REACH : REACH + rows, PAD : PAD + cols] = own[...]
    zero[REACH : REACH + rows, PAD - REACH : PAD] = left[...]
    zero[REACH : REACH + rows, PAD + cols : PAD + cols + REACH] = right[...]

    @pl.when(band % 2 == 0)
    def _():
        zero[0:REACH, wide] = jnp.where(band > 0, outer[...], 0.0)
        zero[REACH + rows : deep, wide] = inner[...]

    @pl.when(band % 2 == 1)
    def _():
        zero[0:REACH, wide] = inner[...]
        zero[REACH + rows : deep, wide] = jnp.where(band < 15, outer[...], 0.0)

    def masks(size):
        lane = lax.broadcasted_iota(jnp.int32, (size, lanes), 1)
        return {1: lane < lanes - 1, -1: lane >= 1, 2: lane < lanes - 2, -2: lane >= 2}

    def advance(source, target, edge, unroll, twice=None):
        start = PAD - REACH + edge
        size = cols + 2 * (REACH - edge)
        inside = masks(size)
        at = lax.broadcasted_iota(jnp.int32, (size, lanes), 0) + (start - PAD)
        col_in = (at >= -space * cols) & (at < (8 - space) * cols)
        beside = jnp.where((at < 0) | (at >= cols), 2.0, 1.0)

        def step(i, carry):
            for j in range(unroll):
                r = edge + unroll * i + j
                own = r - REACH
                row_in = (own >= -band * rows) & (own < (16 - band) * rows)
                image = jnp.where(col_in & row_in, laplacian(source, r, start, size, inside), 0.0)
                target[r, start : start + size] = image
                if twice is not None:
                    twice[r, start : start + size] = image * jnp.where((own < 0) | (own >= rows), 2.0, beside)
            return carry

        lax.fori_loop(0, (deep - 2 * edge) // unroll, step, 0)

    blank = jnp.zeros((cols + 2 * PAD, lanes), F32)
    for r in (REACH - 2, REACH + rows + 1):
        double[r] = blank
    for r in range(REACH - 1, REACH + rows + 1):
        double[r, 0:PAD] = blank[0:PAD]
        double[r, PAD + cols :] = blank[0:PAD]
    advance(zero, one, 2, 7)
    advance(one, two, 4, 5, double)
    inside = masks(cols)

    def fold(p, q):
        product = p * q
        return functools.reduce(lambda a, b: a + b, [product[i : i + 8] for i in range(0, cols, 8)])

    def gather(i, sums):
        for j in range(4):
            r = 4 * i + j
            at = r + REACH
            s0 = zero[at, PAD : PAD + cols]
            s1 = one[at, PAD : PAD + cols]
            s2 = two[at, PAD : PAD + cols]
            s3 = laplacian(two, at, PAD, cols, inside, double)
            first_out[r] = s1
            second_out[r] = s2
            pairs = ((s0, s0), (s0, s1), (s1, s1), (s1, s2), (s2, s2), (s2, s3))
            sums = tuple(t + fold(p, q) for t, (p, q) in zip(sums, pairs))
        return sums

    sums = lax.fori_loop(0, rows // 4, gather, tuple(jnp.zeros((8, lanes), F32) for _ in range(2 * ITERS)))
    spot = lax.broadcasted_iota(jnp.int32, (1, lanes), 1)
    line = jnp.zeros((1, lanes), F32)
    for k, part in enumerate(sums):
        whole = jnp.sum(jnp.sum(part, axis=0, keepdims=True), axis=1, keepdims=True)
        line = line + jnp.where(spot == k, whole, 0.0)
    lines[...] = jnp.broadcast_to(line, lines.shape)


def krylov(own, pieces):
    rows, cols, lanes = own.shape
    scratch = pltpu.VMEM((rows + 2 * REACH, cols + 2 * PAD, lanes), F32)
    vmem = pl.BlockSpec(memory_space=pltpu.VMEM)
    field = jax.ShapeDtypeStruct(own.shape, F32)
    return pl.pallas_call(
        krylov_body,
        out_shape=(field, field, jax.ShapeDtypeStruct((128, lanes), F32)),
        in_specs=[vmem] * (1 + len(pieces)),
        out_specs=(vmem, vmem, vmem),
        scratch_shapes=[scratch] * 4,
        compiler_params=pltpu.CompilerParams(vmem_limit_bytes=8 * 2**20),
        name="krylov",
    )(own, *pieces)


def weights_of(moments):
    unit = [m / moments[0] * 0.125**k for k, m in enumerate(moments)]

    def inner(a, b, shift):
        terms = [x * y * unit[i + j + shift] for i, x in enumerate(a) for j, y in enumerate(b)]
        return functools.reduce(lambda p, q: p + q, terms)

    residual, direction, answer = [1.0], [1.0], []
    norm = unit[0]
    for step in range(ITERS):
        alpha = norm / inner(direction, direction, 1)
        old = answer + [0.0] * (len(direction) - len(answer))
        answer = [a + alpha * d for a, d in zip(old, direction)]
        if step + 1 < ITERS:
            residual = [r - alpha * d for r, d in zip(residual + [0.0], [0.0] + direction)]
            fresh = inner(residual, residual, 0)
            ratio = fresh / norm
            direction = [r + ratio * d for r, d in zip(residual, direction + [0.0])]
            norm = fresh
    return [a * 0.125 ** (k + 1) for k, a in enumerate(answer)]


def combine_body(lines, own, first, second, out):
    line = jnp.sum(lines[...], axis=0, keepdims=True)
    spot = lax.broadcasted_iota(jnp.int32, line.shape, 1)
    moments = [jnp.sum(jnp.where(spot == k, line, 0.0), axis=1, keepdims=True) for k in range(2 * ITERS)]
    factors = [jnp.broadcast_to(f, own.shape[1:]) for f in weights_of(moments)]
    for r in range(own.shape[0]):
        out[r] = factors[0] * own[r] + factors[1] * first[r] + factors[2] * second[r]


def combine(lines, own, first, second):
    vmem = pl.BlockSpec(memory_space=pltpu.VMEM)
    return pl.pallas_call(
        combine_body,
        out_shape=jax.ShapeDtypeStruct(own.shape, F32),
        in_specs=[vmem] * 4,
        out_specs=vmem,
        compiler_params=pltpu.CompilerParams(vmem_limit_bytes=8 * 2**20),
        name="combine",
    )(lines, own, first, second)


def local(orbitals, occupations):
    scale = 4.0 * math.pi / (orbitals.shape[0] * 16)
    source = own_density(orbitals, occupations, scale)
    first, second, lines = krylov(source, halo(source))
    lines = lax.all_to_all(lines[:, None], EVERY, split_axis=0, concat_axis=0, tiled=True)[:, 0]
    return combine(lines, source, first, second)


def solution(mesh):
    split = Mesh(mesh.devices.reshape(SIDE, SIDE, SIDE, 2), EVERY)
    in_specs = (P(BAND, None, SPACE, None), P(BAND))
    out_specs = P(BAND, SPACE, None)
    return jax.shard_map(local, mesh=split, in_specs=in_specs, out_specs=out_specs, check_vma=False)
```

```python
import functools
import math

import jax
import jax.numpy as jnp
from jax import lax
from jax.experimental import pallas as pl
from jax.experimental.pallas import tpu as pltpu
from jax.sharding import Mesh
from jax.sharding import PartitionSpec as P


ITERS = 3
REACH = 2 * ITERS - 1
SIDEWAYS = REACH - 1
BAND = ("band_0", "band_1")
SPACE = ("space_0", "space_1")
EVERY = BAND + SPACE
SIDE = 4
F32 = jnp.float32


def device(z, x, y, core):
    return ((z * SIDE + x) * SIDE + y) * 2 + core


def moves(target):
    places = [(z, x, y, c) for z in range(SIDE) for x in range(SIDE) for y in range(SIDE) for c in range(2)]
    return [(device(*p), device(*target(*p))) for p in places]


def partner(phase, k):
    def target(z, x, y, c):
        if (c == 0) == (phase == 0):
            return z, x ^ k, y, c
        return z ^ k, x, y, c

    return moves(target)


def send(value, pairs):
    return lax.ppermute(value, EVERY, pairs)


CHUNK = 160


def density_body(firsts, scale, orb, occ, *refs):
    outs, (held, level, arrive, ready) = refs[:-4], refs[-4:]
    z, x, core = lax.axis_index("band_0"), lax.axis_index("band_1"), lax.axis_index("space_1")
    bands, deep = held.shape[1:3]
    weights = pltpu.make_async_copy(occ, level, ready)
    copies = []
    for slot in range(len(firsts) * SIDE):
        first, second = firsts[slot // SIDE], slot % SIDE
        to_z = z ^ jnp.where(core == 0, second, first)
        to_x = x ^ jnp.where(core == 0, first, second)
        row = pl.multiple_of((to_z * SIDE + to_x) * deep, deep)
        copies.append(pltpu.make_async_copy(orb.at[:, pl.ds(row, deep)], held.at[slot], arrive.at[slot]))
        copies[-1].start()
        if slot == 0:
            weights.start()
    weights.wait()
    factor = [level[b] * scale for b in range(bands)]
    for slot, copy in enumerate(copies):
        copy.wait()
        out, at = outs[slot // 2], slot % 2

        def part(i, carry):
            rows = pl.ds(pl.multiple_of(i * CHUNK, CHUNK), CHUNK)
            total = None
            for b in range(bands):
                wave = held[slot, b, rows].astype(F32)
                term = factor[b] * wave * wave
                total = term if total is None else total + term
            out[at, rows] = total
            return carry

        lax.fori_loop(0, deep // CHUNK, part, 0)


def density_part(orbitals, occupations, scale, firsts):
    bands, rows, cols, lanes = orbitals.shape
    deep = rows // 16
    slots = len(firsts) * SIDE
    half = jax.ShapeDtypeStruct((SIDE // 2, deep * cols, lanes), F32)
    vmem = pl.BlockSpec(memory_space=pltpu.VMEM)
    hbm = pl.BlockSpec(memory_space=pl.ANY)
    parts = pl.pallas_call(
        functools.partial(density_body, firsts, scale),
        out_shape=(half,) * (2 * len(firsts)),
        in_specs=[hbm, hbm],
        out_specs=(vmem,) * (2 * len(firsts)),
        scratch_shapes=[
            pltpu.VMEM((slots, bands, deep * cols, lanes), orbitals.dtype),
            pltpu.SMEM((bands,), F32),
            pltpu.SemaphoreType.DMA((slots,)),
            pltpu.SemaphoreType.DMA,
        ],
        compiler_params=pltpu.CompilerParams(vmem_limit_bytes=52 * 2**20),
        cost_estimate=pl.CostEstimate(flops=0, bytes_accessed=orbitals.size // 2, transcendentals=0),
        name="density",
    )(orbitals.reshape(bands, rows * cols, lanes), occupations)
    return [p.reshape(SIDE // 2, deep, cols, lanes) for p in parts]


def own_density(orbitals, occupations, scale):
    a2, b2 = density_part(orbitals, occupations, scale, (2,))
    a_near, b_near = send(a2, partner(0, 1)), send(b2, partner(0, 3))
    a1, b1, a3, b3 = density_part(orbitals, occupations, scale, (1, 3))
    a_first, b_first = send(a1, partner(0, 1)), send(b3, partner(0, 3))
    a_near, b_near = lax.optimization_barrier((a_near, b_near))
    b1, a3 = b1 + b_near, a3 + a_near
    b1, a3, late = lax.optimization_barrier((b1, a3, occupations))
    b_last, a_last = send(b1, partner(0, 1)), send(a3, partner(0, 3))
    a0, b0 = density_part(orbitals, late, scale, (0,))
    a_first, a_last, b_first, b_last = lax.optimization_barrier((a_first, a_last, b_first, b_last))
    a0, b0 = a0 + a_first + a_last, b0 + b_first + b_last
    total = a0[0]
    for block, k in ((a0[1], 1), (b0[1], 3), (b0[0], 2)):
        total = total + send(block, partner(1, k))
    return total


def across(y, core):
    space = 2 * y + core
    space = (space + 1 if core else space - 1) % 8
    return space // 2, space % 2


def beside():
    pairs = []
    for z in range(SIDE):
        for x in range(SIDE):
            for y in range(SIDE):
                for c in range(2):
                    pairs.append((device(z, x, y, c), device(z, x, *across(y, c))))
    return pairs


def halo(field):
    first = lax.axis_index("space_1") == 0
    left, right = field[:, :REACH], field[:, -REACH:]
    far = send(jnp.where(first, left, right), beside())
    near = lax.ppermute(jnp.where(first, right, left), "space_1", [(0, 1), (1, 0)])
    space = lax.axis_index(SPACE)
    far = jnp.where((space > 0) & (space < 7), far, 0.0)
    left, right = jnp.where(first, far, near), jnp.where(first, near, far)
    wide = jnp.concatenate([left[:, -SIDEWAYS:], field, right[:, :SIDEWAYS]], 1)
    even = lax.axis_index("band_1") % 2 == 0
    inner = [(i, i ^ 1) for i in range(16)]
    outer = [(i, (i + 1 if i % 2 else i - 1) % 16) for i in range(16)]
    first_rows, last_rows = wide[:REACH], wide[-REACH:]
    inner = lax.ppermute(jnp.where(even, last_rows, first_rows), BAND, inner)
    outer = lax.ppermute(jnp.where(even, first_rows, last_rows), BAND, outer)
    return left, right, inner, outer


def laplacian(ref, r, start, size, masks, outer=None):
    outer = ref if outer is None else outer

    def at(down, across):
        source = outer if abs(down) + abs(across) == 2 else ref
        return source[r + down, start + across : start + across + size]

    center = at(0, 0)
    lanes = center.shape[1]

    def along(k):
        return jnp.where(masks[k], pltpu.roll(center, -k % lanes, 1), 0.0)

    near = at(1, 0) + at(-1, 0) + at(0, 1) + at(0, -1) + along(1) + along(-1)
    distant = at(2, 0) + at(-2, 0) + at(0, 2) + at(0, -2) + along(2) + along(-2)
    return 7.5 * center - 4.0 / 3.0 * near + 1.0 / 12.0 * distant


PAD = 8


def krylov_body(own, left, right, inner, outer, first_out, second_out, lines, zero, one, two, double):
    rows, cols, lanes = own.shape
    deep = rows + 2 * REACH
    band, space = lax.axis_index(BAND), lax.axis_index(SPACE)
    wide = slice(PAD - SIDEWAYS, PAD + cols + SIDEWAYS)
    for edge in (slice(0, REACH), slice(REACH + rows, deep)):
        zero[edge, 0:PAD] = jnp.zeros((REACH, PAD, lanes), F32)
        zero[edge, PAD + cols :] = jnp.zeros((REACH, PAD, lanes), F32)
    zero[REACH : REACH + rows, PAD : PAD + cols] = own[...]
    zero[REACH : REACH + rows, PAD - REACH : PAD] = left[...]
    zero[REACH : REACH + rows, PAD + cols : PAD + cols + REACH] = right[...]

    @pl.when(band % 2 == 0)
    def _():
        zero[0:REACH, wide] = jnp.where(band > 0, outer[...], 0.0)
        zero[REACH + rows : deep, wide] = inner[...]

    @pl.when(band % 2 == 1)
    def _():
        zero[0:REACH, wide] = inner[...]
        zero[REACH + rows : deep, wide] = jnp.where(band < 15, outer[...], 0.0)

    def masks(size):
        lane = lax.broadcasted_iota(jnp.int32, (size, lanes), 1)
        return {1: lane < lanes - 1, -1: lane >= 1, 2: lane < lanes - 2, -2: lane >= 2}

    def advance(source, target, edge, unroll, twice=None):
        start = PAD - REACH + edge
        size = cols + 2 * (REACH - edge)
        inside = masks(size)
        at = lax.broadcasted_iota(jnp.int32, (size, lanes), 0) + (start - PAD)
        col_in = (at >= -space * cols) & (at < (8 - space) * cols)
        beside = jnp.where((at < 0) | (at >= cols), 2.0, 1.0)

        def step(i, carry):
            for j in range(unroll):
                r = edge + unroll * i + j
                own = r - REACH
                row_in = (own >= -band * rows) & (own < (16 - band) * rows)
                image = jnp.where(col_in & row_in, laplacian(source, r, start, size, inside), 0.0)
                target[r, start : start + size] = image
                if twice is not None:
                    twice[r, start : start + size] = image * jnp.where((own < 0) | (own >= rows), 2.0, beside)
            return carry

        lax.fori_loop(0, (deep - 2 * edge) // unroll, step, 0)

    blank = jnp.zeros((cols + 2 * PAD, lanes), F32)
    for r in (REACH - 2, REACH + rows + 1):
        double[r] = blank
    for r in range(REACH - 1, REACH + rows + 1):
        double[r, 0:PAD] = blank[0:PAD]
        double[r, PAD + cols :] = blank[0:PAD]
    advance(zero, one, 2, 7)
    advance(one, two, 4, 5, double)
    inside = masks(cols)

    def fold(p, q):
        product = p * q
        return functools.reduce(lambda a, b: a + b, [product[i : i + 8] for i in range(0, cols, 8)])

    def gather(i, sums):
        for j in range(4):
            r = 4 * i + j
            at = r + REACH
            s0 = zero[at, PAD : PAD + cols]
            s1 = one[at, PAD : PAD + cols]
            s2 = two[at, PAD : PAD + cols]
            s3 = laplacian(two, at, PAD, cols, inside, double)
            first_out[r] = s1
            second_out[r] = s2
            pairs = ((s0, s0), (s0, s1), (s1, s1), (s1, s2), (s2, s2), (s2, s3))
            sums = tuple(t + fold(p, q) for t, (p, q) in zip(sums, pairs))
        return sums

    sums = lax.fori_loop(0, rows // 4, gather, tuple(jnp.zeros((8, lanes), F32) for _ in range(2 * ITERS)))
    spot = lax.broadcasted_iota(jnp.int32, (1, lanes), 1)
    line = jnp.zeros((1, lanes), F32)
    for k, part in enumerate(sums):
        whole = jnp.sum(jnp.sum(part, axis=0, keepdims=True), axis=1, keepdims=True)
        line = line + jnp.where(spot == k, whole, 0.0)
    lines[...] = jnp.broadcast_to(line, lines.shape)


def krylov(own, pieces):
    rows, cols, lanes = own.shape
    scratch = pltpu.VMEM((rows + 2 * REACH, cols + 2 * PAD, lanes), F32)
    vmem = pl.BlockSpec(memory_space=pltpu.VMEM)
    field = jax.ShapeDtypeStruct(own.shape, F32)
    return pl.pallas_call(
        krylov_body,
        out_shape=(field, field, jax.ShapeDtypeStruct((128, lanes), F32)),
        in_specs=[vmem] * (1 + len(pieces)),
        out_specs=(vmem, vmem, vmem),
        scratch_shapes=[scratch] * 4,
        compiler_params=pltpu.CompilerParams(vmem_limit_bytes=8 * 2**20),
        name="krylov",
    )(own, *pieces)


def weights_of(moments):
    unit = [m / moments[0] * 0.125**k for k, m in enumerate(moments)]

    def inner(a, b, shift):
        terms = [x * y * unit[i + j + shift] for i, x in enumerate(a) for j, y in enumerate(b)]
        return functools.reduce(lambda p, q: p + q, terms)

    residual, direction, answer = [1.0], [1.0], []
    norm = unit[0]
    for step in range(ITERS):
        alpha = norm / inner(direction, direction, 1)
        old = answer + [0.0] * (len(direction) - len(answer))
        answer = [a + alpha * d for a, d in zip(old, direction)]
        if step + 1 < ITERS:
            residual = [r - alpha * d for r, d in zip(residual + [0.0], [0.0] + direction)]
            fresh = inner(residual, residual, 0)
            ratio = fresh / norm
            direction = [r + ratio * d for r, d in zip(residual, direction + [0.0])]
            norm = fresh
    return [a * 0.125 ** (k + 1) for k, a in enumerate(answer)]


def combine_body(lines, own, first, second, out):
    line = jnp.sum(lines[...], axis=0, keepdims=True)
    spot = lax.broadcasted_iota(jnp.int32, line.shape, 1)
    moments = [jnp.sum(jnp.where(spot == k, line, 0.0), axis=1, keepdims=True) for k in range(2 * ITERS)]
    factors = [jnp.broadcast_to(f, own.shape[1:]) for f in weights_of(moments)]
    for r in range(own.shape[0]):
        out[r] = factors[0] * own[r] + factors[1] * first[r] + factors[2] * second[r]


def combine(lines, own, first, second):
    vmem = pl.BlockSpec(memory_space=pltpu.VMEM)
    return pl.pallas_call(
        combine_body,
        out_shape=jax.ShapeDtypeStruct(own.shape, F32),
        in_specs=[vmem] * 4,
        out_specs=vmem,
        compiler_params=pltpu.CompilerParams(vmem_limit_bytes=8 * 2**20),
        name="combine",
    )(lines, own, first, second)


def local(orbitals, occupations):
    scale = 4.0 * math.pi / (orbitals.shape[0] * 16)
    source = own_density(orbitals, occupations, scale)
    first, second, lines = krylov(source, halo(source))
    lines = lax.all_to_all(lines[:, None], EVERY, split_axis=0, concat_axis=0, tiled=True)[:, 0]
    return combine(lines, source, first, second)


def solution(mesh):
    split = Mesh(mesh.devices.reshape(SIDE, SIDE, SIDE, 2), EVERY)
    in_specs = (P(BAND, None, SPACE, None), P(BAND))
    out_specs = P(BAND, SPACE, None)
    return jax.shard_map(local, mesh=split, in_specs=in_specs, out_specs=out_specs, check_vma=False)
```

```python
import functools
import math

import jax
import jax.numpy as jnp
from jax import lax
from jax.experimental import pallas as pl
from jax.experimental.pallas import tpu as pltpu
from jax.sharding import Mesh
from jax.sharding import PartitionSpec as P


ITERS = 3
REACH = 2 * ITERS - 1
SIDEWAYS = REACH - 1
BAND = ("band_0", "band_1")
SPACE = ("space_0", "space_1")
EVERY = BAND + SPACE
SIDE = 4
F32 = jnp.float32


def device(z, x, y, core):
    return ((z * SIDE + x) * SIDE + y) * 2 + core


def moves(target):
    places = [(z, x, y, c) for z in range(SIDE) for x in range(SIDE) for y in range(SIDE) for c in range(2)]
    return [(device(*p), device(*target(*p))) for p in places]


def partner(phase, k):
    def target(z, x, y, c):
        if (c == 0) == (phase == 0):
            return z, x ^ k, y, c
        return z ^ k, x, y, c

    return moves(target)


def send(value, pairs):
    return lax.ppermute(value, EVERY, pairs)


CHUNK = 160


def density_body(firsts, scale, orb, occ, *refs):
    outs, (held, level, arrive, ready) = refs[:-4], refs[-4:]
    z, x, core = lax.axis_index("band_0"), lax.axis_index("band_1"), lax.axis_index("space_1")
    bands, deep = held.shape[1:3]
    weights = pltpu.make_async_copy(occ, level, ready)
    copies = []
    for slot in range(len(firsts) * SIDE):
        first, second = firsts[slot // SIDE], slot % SIDE
        to_z = z ^ jnp.where(core == 0, second, first)
        to_x = x ^ jnp.where(core == 0, first, second)
        row = pl.multiple_of((to_z * SIDE + to_x) * deep, deep)
        copies.append(pltpu.make_async_copy(orb.at[:, pl.ds(row, deep)], held.at[slot], arrive.at[slot]))
        copies[-1].start()
        if slot == 0:
            weights.start()
    weights.wait()
    factor = [level[b] * scale for b in range(bands)]
    for slot, copy in enumerate(copies):
        copy.wait()
        out, at = outs[slot // 2], slot % 2

        def part(i, carry):
            rows = pl.ds(pl.multiple_of(i * CHUNK, CHUNK), CHUNK)
            total = None
            for b in range(bands):
                wave = held[slot, b, rows].astype(F32)
                term = factor[b] * wave * wave
                total = term if total is None else total + term
            out[at, rows] = total
            return carry

        lax.fori_loop(0, deep // CHUNK, part, 0)


def density_part(orbitals, occupations, scale, firsts):
    bands, rows, cols, lanes = orbitals.shape
    deep = rows // 16
    slots = len(firsts) * SIDE
    half = jax.ShapeDtypeStruct((SIDE // 2, deep * cols, lanes), F32)
    vmem = pl.BlockSpec(memory_space=pltpu.VMEM)
    hbm = pl.BlockSpec(memory_space=pl.ANY)
    parts = pl.pallas_call(
        functools.partial(density_body, firsts, scale),
        out_shape=(half,) * (2 * len(firsts)),
        in_specs=[hbm, hbm],
        out_specs=(vmem,) * (2 * len(firsts)),
        scratch_shapes=[
            pltpu.VMEM((slots, bands, deep * cols, lanes), orbitals.dtype),
            pltpu.SMEM((bands,), F32),
            pltpu.SemaphoreType.DMA((slots,)),
            pltpu.SemaphoreType.DMA,
        ],
        compiler_params=pltpu.CompilerParams(vmem_limit_bytes=52 * 2**20),
        cost_estimate=pl.CostEstimate(flops=0, bytes_accessed=orbitals.size // 2, transcendentals=0),
        name="density",
    )(orbitals.reshape(bands, rows * cols, lanes), occupations)
    return [p.reshape(SIDE // 2, deep, cols, lanes) for p in parts]


def own_density(orbitals, occupations, scale):
    a2, b2 = density_part(orbitals, occupations, scale, (2,))
    a_near, b_near = send(a2, partner(0, 1)), send(b2, partner(0, 3))
    a1, b1, a3, b3 = density_part(orbitals, occupations, scale, (1, 3))
    a_first, b_first = send(a1, partner(0, 1)), send(b3, partner(0, 3))
    a_near, b_near = lax.optimization_barrier((a_near, b_near))
    b1, a3 = b1 + b_near, a3 + a_near
    b1, a3, late = lax.optimization_barrier((b1, a3, occupations))
    b_last, a_last = send(b1, partner(0, 1)), send(a3, partner(0, 3))
    a0, b0 = density_part(orbitals, late, scale, (0,))
    a_first, a_last, b_first, b_last = lax.optimization_barrier((a_first, a_last, b_first, b_last))
    a0, b0 = a0 + a_first + a_last, b0 + b_first + b_last
    total = a0[0]
    for block, k in ((a0[1], 1), (b0[1], 3), (b0[0], 2)):
        total = total + send(block, partner(1, k))
    return total


def across(y, core):
    space = 2 * y + core
    space = (space + 1 if core else space - 1) % 8
    return space // 2, space % 2


def beside():
    pairs = []
    for z in range(SIDE):
        for x in range(SIDE):
            for y in range(SIDE):
                for c in range(2):
                    pairs.append((device(z, x, y, c), device(z, x, *across(y, c))))
    return pairs


def halo(field):
    first = lax.axis_index("space_1") == 0
    left, right = field[:, :REACH], field[:, -REACH:]
    space = lax.axis_index(SPACE)
    border = jnp.where(first, left, right)
    far = send(jnp.where((space > 0) & (space < 7), border, 0.0), beside())
    near = lax.ppermute(jnp.where(first, right, left), "space_1", [(0, 1), (1, 0)])
    left, right = jnp.where(first, far, near), jnp.where(first, near, far)
    wide = jnp.concatenate([left[:, -SIDEWAYS:], field, right[:, :SIDEWAYS]], 1)
    even = lax.axis_index("band_1") % 2 == 0
    inner = [(i, i ^ 1) for i in range(16)]
    outer = [(i, (i + 1 if i % 2 else i - 1) % 16) for i in range(16)]
    first_rows, last_rows = wide[:REACH], wide[-REACH:]
    inner = lax.ppermute(jnp.where(even, last_rows, first_rows), BAND, inner)
    outer = lax.ppermute(jnp.where(even, first_rows, last_rows), BAND, outer)
    return left, right, inner, outer


def laplacian(ref, r, start, size, masks, outer=None):
    outer = ref if outer is None else outer

    def at(down, across):
        source = outer if abs(down) + abs(across) == 2 else ref
        return source[r + down, start + across : start + across + size]

    center = at(0, 0)
    lanes = center.shape[1]

    def along(k):
        return jnp.where(masks[k], pltpu.roll(center, -k % lanes, 1), 0.0)

    near = at(1, 0) + at(-1, 0) + at(0, 1) + at(0, -1) + along(1) + along(-1)
    distant = at(2, 0) + at(-2, 0) + at(0, 2) + at(0, -2) + along(2) + along(-2)
    return 7.5 * center - 4.0 / 3.0 * near + 1.0 / 12.0 * distant


PAD = 8


def krylov_body(own, left, right, inner, outer, first_out, second_out, lines, zero, one, two, double):
    rows, cols, lanes = own.shape
    deep = rows + 2 * REACH
    band, space = lax.axis_index(BAND), lax.axis_index(SPACE)
    wide = slice(PAD - SIDEWAYS, PAD + cols + SIDEWAYS)
    for edge in (slice(0, REACH), slice(REACH + rows, deep)):
        zero[edge, 0:PAD] = jnp.zeros((REACH, PAD, lanes), F32)
        zero[edge, PAD + cols :] = jnp.zeros((REACH, PAD, lanes), F32)
    zero[REACH : REACH + rows, PAD : PAD + cols] = own[...]
    zero[REACH : REACH + rows, PAD - REACH : PAD] = left[...]
    zero[REACH : REACH + rows, PAD + cols : PAD + cols + REACH] = right[...]

    @pl.when(band % 2 == 0)
    def _():
        zero[0:REACH, wide] = jnp.where(band > 0, outer[...], 0.0)
        zero[REACH + rows : deep, wide] = inner[...]

    @pl.when(band % 2 == 1)
    def _():
        zero[0:REACH, wide] = inner[...]
        zero[REACH + rows : deep, wide] = jnp.where(band < 15, outer[...], 0.0)

    def masks(size):
        lane = lax.broadcasted_iota(jnp.int32, (size, lanes), 1)
        return {1: lane < lanes - 1, -1: lane >= 1, 2: lane < lanes - 2, -2: lane >= 2}

    def advance(source, target, edge, unroll, twice=None):
        start = PAD - REACH + edge
        size = cols + 2 * (REACH - edge)
        inside = masks(size)
        at = lax.broadcasted_iota(jnp.int32, (size, lanes), 0) + (start - PAD)
        col_in = (at >= -space * cols) & (at < (8 - space) * cols)
        beside = jnp.where((at < 0) | (at >= cols), 2.0, 1.0)

        def step(i, carry):
            for j in range(unroll):
                r = edge + unroll * i + j
                own = r - REACH
                row_in = (own >= -band * rows) & (own < (16 - band) * rows)
                image = jnp.where(col_in & row_in, laplacian(source, r, start, size, inside), 0.0)
                target[r, start : start + size] = image
                if twice is not None:
                    twice[r, start : start + size] = image * jnp.where((own < 0) | (own >= rows), 2.0, beside)
            return carry

        lax.fori_loop(0, (deep - 2 * edge) // unroll, step, 0)

    blank = jnp.zeros((cols + 2 * PAD, lanes), F32)
    for r in (REACH - 2, REACH + rows + 1):
        double[r] = blank
    for r in range(REACH - 1, REACH + rows + 1):
        double[r, 0:PAD] = blank[0:PAD]
        double[r, PAD + cols :] = blank[0:PAD]
    advance(zero, one, 2, 7)
    advance(one, two, 4, 5, double)
    inside = masks(cols)

    def fold(p, q):
        product = p * q
        return functools.reduce(lambda a, b: a + b, [product[i : i + 8] for i in range(0, cols, 8)])

    def gather(i, sums):
        for j in range(4):
            r = 4 * i + j
            at = r + REACH
            s0 = zero[at, PAD : PAD + cols]
            s1 = one[at, PAD : PAD + cols]
            s2 = two[at, PAD : PAD + cols]
            s3 = laplacian(two, at, PAD, cols, inside, double)
            first_out[r] = s1
            second_out[r] = s2
            pairs = ((s0, s0), (s0, s1), (s1, s1), (s1, s2), (s2, s2), (s2, s3))
            sums = tuple(t + fold(p, q) for t, (p, q) in zip(sums, pairs))
        return sums

    sums = lax.fori_loop(0, rows // 4, gather, tuple(jnp.zeros((8, lanes), F32) for _ in range(2 * ITERS)))
    spot = lax.broadcasted_iota(jnp.int32, (1, lanes), 1)
    line = jnp.zeros((1, lanes), F32)
    for k, part in enumerate(sums):
        whole = jnp.sum(jnp.sum(part, axis=0, keepdims=True), axis=1, keepdims=True)
        line = line + jnp.where(spot == k, whole, 0.0)
    lines[...] = jnp.broadcast_to(line, lines.shape)


def krylov(own, pieces):
    rows, cols, lanes = own.shape
    scratch = pltpu.VMEM((rows + 2 * REACH, cols + 2 * PAD, lanes), F32)
    vmem = pl.BlockSpec(memory_space=pltpu.VMEM)
    field = jax.ShapeDtypeStruct(own.shape, F32)
    return pl.pallas_call(
        krylov_body,
        out_shape=(field, field, jax.ShapeDtypeStruct((128, lanes), F32)),
        in_specs=[vmem] * (1 + len(pieces)),
        out_specs=(vmem, vmem, vmem),
        scratch_shapes=[scratch] * 4,
        compiler_params=pltpu.CompilerParams(vmem_limit_bytes=8 * 2**20),
        name="krylov",
    )(own, *pieces)


def weights_of(moments):
    unit = [m / moments[0] * 0.125**k for k, m in enumerate(moments)]

    def inner(a, b, shift):
        terms = [x * y * unit[i + j + shift] for i, x in enumerate(a) for j, y in enumerate(b)]
        return functools.reduce(lambda p, q: p + q, terms)

    residual, direction, answer = [1.0], [1.0], []
    norm = unit[0]
    for step in range(ITERS):
        alpha = norm / inner(direction, direction, 1)
        old = answer + [0.0] * (len(direction) - len(answer))
        answer = [a + alpha * d for a, d in zip(old, direction)]
        if step + 1 < ITERS:
            residual = [r - alpha * d for r, d in zip(residual + [0.0], [0.0] + direction)]
            fresh = inner(residual, residual, 0)
            ratio = fresh / norm
            direction = [r + ratio * d for r, d in zip(residual, direction + [0.0])]
            norm = fresh
    return [a * 0.125 ** (k + 1) for k, a in enumerate(answer)]


def combine_body(lines, own, first, second, out):
    line = jnp.sum(lines[...], axis=0, keepdims=True)
    spot = lax.broadcasted_iota(jnp.int32, line.shape, 1)
    moments = [jnp.sum(jnp.where(spot == k, line, 0.0), axis=1, keepdims=True) for k in range(2 * ITERS)]
    factors = [jnp.broadcast_to(f, own.shape[1:]) for f in weights_of(moments)]
    for r in range(own.shape[0]):
        out[r] = factors[0] * own[r] + factors[1] * first[r] + factors[2] * second[r]


def combine(lines, own, first, second):
    vmem = pl.BlockSpec(memory_space=pltpu.VMEM)
    return pl.pallas_call(
        combine_body,
        out_shape=jax.ShapeDtypeStruct(own.shape, F32),
        in_specs=[vmem] * 4,
        out_specs=vmem,
        compiler_params=pltpu.CompilerParams(vmem_limit_bytes=8 * 2**20),
        name="combine",
    )(lines, own, first, second)


def local(orbitals, occupations):
    scale = 4.0 * math.pi / (orbitals.shape[0] * 16)
    source = own_density(orbitals, occupations, scale)
    first, second, lines = krylov(source, halo(source))
    lines = lax.all_to_all(lines[:, None], EVERY, split_axis=0, concat_axis=0, tiled=True)[:, 0]
    return combine(lines, source, first, second)


def solution(mesh):
    split = Mesh(mesh.devices.reshape(SIDE, SIDE, SIDE, 2), EVERY)
    in_specs = (P(BAND, None, SPACE, None), P(BAND))
    out_specs = P(BAND, SPACE, None)
    return jax.shard_map(local, mesh=split, in_specs=in_specs, out_specs=out_specs, check_vma=False)
```

```python
import functools
import math

import jax
import jax.numpy as jnp
from jax import lax
from jax.experimental import pallas as pl
from jax.experimental.pallas import tpu as pltpu
from jax.sharding import Mesh
from jax.sharding import PartitionSpec as P


ITERS = 3
REACH = 2 * ITERS - 1
SIDEWAYS = REACH - 1
BAND = ("band_0", "band_1")
SPACE = ("space_0", "space_1")
EVERY = BAND + SPACE
SIDE = 4
F32 = jnp.float32


def device(z, x, y, core):
    return ((z * SIDE + x) * SIDE + y) * 2 + core


def moves(target):
    places = [(z, x, y, c) for z in range(SIDE) for x in range(SIDE) for y in range(SIDE) for c in range(2)]
    return [(device(*p), device(*target(*p))) for p in places]


def partner(phase, k):
    def target(z, x, y, c):
        if (c == 0) == (phase == 0):
            return z, x ^ k, y, c
        return z ^ k, x, y, c

    return moves(target)


def send(value, pairs):
    return lax.ppermute(value, EVERY, pairs)


CHUNK = 160


def density_body(firsts, scale, orb, occ, *refs):
    outs, (held, level, arrive, ready) = refs[:-4], refs[-4:]
    z, x, core = lax.axis_index("band_0"), lax.axis_index("band_1"), lax.axis_index("space_1")
    bands, deep = held.shape[1:3]
    weights = pltpu.make_async_copy(occ, level, ready)
    copies = []
    for slot in range(len(firsts) * SIDE):
        first, second = firsts[slot // SIDE], slot % SIDE
        to_z = z ^ jnp.where(core == 0, second, first)
        to_x = x ^ jnp.where(core == 0, first, second)
        row = pl.multiple_of((to_z * SIDE + to_x) * deep, deep)
        copies.append(pltpu.make_async_copy(orb.at[:, pl.ds(row, deep)], held.at[slot], arrive.at[slot]))
        copies[-1].start()
        if slot == 0:
            weights.start()
    weights.wait()
    factor = [level[b] * scale for b in range(bands)]
    for slot, copy in enumerate(copies):
        copy.wait()
        out, at = outs[slot // 2], slot % 2

        def part(i, carry):
            rows = pl.ds(pl.multiple_of(i * CHUNK, CHUNK), CHUNK)
            total = None
            for b in range(bands):
                wave = held[slot, b, rows].astype(F32)
                term = factor[b] * wave * wave
                total = term if total is None else total + term
            out[at, rows] = total
            return carry

        lax.fori_loop(0, deep // CHUNK, part, 0)


def density_part(orbitals, occupations, scale, firsts):
    bands, rows, cols, lanes = orbitals.shape
    deep = rows // 16
    slots = len(firsts) * SIDE
    half = jax.ShapeDtypeStruct((SIDE // 2, deep * cols, lanes), F32)
    vmem = pl.BlockSpec(memory_space=pltpu.VMEM)
    hbm = pl.BlockSpec(memory_space=pl.ANY)
    parts = pl.pallas_call(
        functools.partial(density_body, firsts, scale),
        out_shape=(half,) * (2 * len(firsts)),
        in_specs=[hbm, hbm],
        out_specs=(vmem,) * (2 * len(firsts)),
        scratch_shapes=[
            pltpu.VMEM((slots, bands, deep * cols, lanes), orbitals.dtype),
            pltpu.SMEM((bands,), F32),
            pltpu.SemaphoreType.DMA((slots,)),
            pltpu.SemaphoreType.DMA,
        ],
        compiler_params=pltpu.CompilerParams(vmem_limit_bytes=52 * 2**20),
        cost_estimate=pl.CostEstimate(flops=0, bytes_accessed=orbitals.size // 2, transcendentals=0),
        name="density",
    )(orbitals.reshape(bands, rows * cols, lanes), occupations)
    return [p.reshape(SIDE // 2, deep, cols, lanes) for p in parts]


def own_density(orbitals, occupations, scale):
    a2, b2 = density_part(orbitals, occupations, scale, (2,))
    a_near, b_near = send(a2, partner(0, 1)), send(b2, partner(0, 3))
    a1, b1, a3, b3 = density_part(orbitals, occupations, scale, (1, 3))
    a_first, b_first = send(a1, partner(0, 1)), send(b3, partner(0, 3))
    token = lax.ppermute(a1[1, :1, :8], "space_1", [(0, 1), (1, 0)])
    a_near, b_near, token = lax.optimization_barrier((a_near, b_near, token))
    b1, a3 = b1 + b_near, a3 + a_near
    b1, a3, late = lax.optimization_barrier((b1, a3, occupations))
    b_last, a_last = send(b1, partner(0, 1)), send(a3, partner(0, 3))
    a0, b0 = density_part(orbitals, late, scale, (0,))
    a_first, a_last, b_first, b_last = lax.optimization_barrier((a_first, a_last, b_first, b_last))
    a0, b0 = a0 + a_first + a_last, b0 + b_first + b_last
    total = a0[0]
    for block, k in ((a0[1], 1), (b0[1], 3), (b0[0], 2)):
        total = total + send(block, partner(1, k))
    return total


def across(y, core):
    space = 2 * y + core
    space = (space + 1 if core else space - 1) % 8
    return space // 2, space % 2


def beside():
    pairs = []
    for z in range(SIDE):
        for x in range(SIDE):
            for y in range(SIDE):
                for c in range(2):
                    pairs.append((device(z, x, y, c), device(z, x, *across(y, c))))
    return pairs


def halo(field):
    first = lax.axis_index("space_1") == 0
    left, right = field[:, :REACH], field[:, -REACH:]
    far = send(jnp.where(first, left, right), beside())
    near = lax.ppermute(jnp.where(first, right, left), "space_1", [(0, 1), (1, 0)])
    space = lax.axis_index(SPACE)
    far = jnp.where((space > 0) & (space < 7), far, 0.0)
    left, right = jnp.where(first, far, near), jnp.where(first, near, far)
    wide = jnp.concatenate([left[:, -SIDEWAYS:], field, right[:, :SIDEWAYS]], 1)
    even = lax.axis_index("band_1") % 2 == 0
    inner = [(i, i ^ 1) for i in range(16)]
    outer = [(i, (i + 1 if i % 2 else i - 1) % 16) for i in range(16)]
    first_rows, last_rows = wide[:REACH], wide[-REACH:]
    inner = lax.ppermute(jnp.where(even, last_rows, first_rows), BAND, inner)
    outer = lax.ppermute(jnp.where(even, first_rows, last_rows), BAND, outer)
    return left, right, inner, outer


def laplacian(ref, r, start, size, masks, outer=None):
    outer = ref if outer is None else outer

    def at(down, across):
        source = outer if abs(down) + abs(across) == 2 else ref
        return source[r + down, start + across : start + across + size]

    center = at(0, 0)
    lanes = center.shape[1]

    def along(k):
        return jnp.where(masks[k], pltpu.roll(center, -k % lanes, 1), 0.0)

    near = at(1, 0) + at(-1, 0) + at(0, 1) + at(0, -1) + along(1) + along(-1)
    distant = at(2, 0) + at(-2, 0) + at(0, 2) + at(0, -2) + along(2) + along(-2)
    return 7.5 * center - 4.0 / 3.0 * near + 1.0 / 12.0 * distant


PAD = 8


def krylov_body(own, left, right, inner, outer, first_out, second_out, lines, zero, one, two, double):
    rows, cols, lanes = own.shape
    deep = rows + 2 * REACH
    band, space = lax.axis_index(BAND), lax.axis_index(SPACE)
    wide = slice(PAD - SIDEWAYS, PAD + cols + SIDEWAYS)
    for edge in (slice(0, REACH), slice(REACH + rows, deep)):
        zero[edge, 0:PAD] = jnp.zeros((REACH, PAD, lanes), F32)
        zero[edge, PAD + cols :] = jnp.zeros((REACH, PAD, lanes), F32)
    zero[REACH : REACH + rows, PAD : PAD + cols] = own[...]
    zero[REACH : REACH + rows, PAD - REACH : PAD] = left[...]
    zero[REACH : REACH + rows, PAD + cols : PAD + cols + REACH] = right[...]

    @pl.when(band % 2 == 0)
    def _():
        zero[0:REACH, wide] = jnp.where(band > 0, outer[...], 0.0)
        zero[REACH + rows : deep, wide] = inner[...]

    @pl.when(band % 2 == 1)
    def _():
        zero[0:REACH, wide] = inner[...]
        zero[REACH + rows : deep, wide] = jnp.where(band < 15, outer[...], 0.0)

    def masks(size):
        lane = lax.broadcasted_iota(jnp.int32, (size, lanes), 1)
        return {1: lane < lanes - 1, -1: lane >= 1, 2: lane < lanes - 2, -2: lane >= 2}

    def advance(source, target, edge, unroll, twice=None):
        start = PAD - REACH + edge
        size = cols + 2 * (REACH - edge)
        inside = masks(size)
        at = lax.broadcasted_iota(jnp.int32, (size, lanes), 0) + (start - PAD)
        col_in = (at >= -space * cols) & (at < (8 - space) * cols)
        beside = jnp.where((at < 0) | (at >= cols), 2.0, 1.0)

        def step(i, carry):
            for j in range(unroll):
                r = edge + unroll * i + j
                own = r - REACH
                row_in = (own >= -band * rows) & (own < (16 - band) * rows)
                image = jnp.where(col_in & row_in, laplacian(source, r, start, size, inside), 0.0)
                target[r, start : start + size] = image
                if twice is not None:
                    twice[r, start : start + size] = image * jnp.where((own < 0) | (own >= rows), 2.0, beside)
            return carry

        lax.fori_loop(0, (deep - 2 * edge) // unroll, step, 0)

    blank = jnp.zeros((cols + 2 * PAD, lanes), F32)
    for r in (REACH - 2, REACH + rows + 1):
        double[r] = blank
    for r in range(REACH - 1, REACH + rows + 1):
        double[r, 0:PAD] = blank[0:PAD]
        double[r, PAD + cols :] = blank[0:PAD]
    advance(zero, one, 2, 7)
    advance(one, two, 4, 5, double)
    inside = masks(cols)

    def fold(p, q):
        product = p * q
        return functools.reduce(lambda a, b: a + b, [product[i : i + 8] for i in range(0, cols, 8)])

    def gather(i, sums):
        for j in range(4):
            r = 4 * i + j
            at = r + REACH
            s0 = zero[at, PAD : PAD + cols]
            s1 = one[at, PAD : PAD + cols]
            s2 = two[at, PAD : PAD + cols]
            s3 = laplacian(two, at, PAD, cols, inside, double)
            first_out[r] = s1
            second_out[r] = s2
            pairs = ((s0, s0), (s0, s1), (s1, s1), (s1, s2), (s2, s2), (s2, s3))
            sums = tuple(t + fold(p, q) for t, (p, q) in zip(sums, pairs))
        return sums

    sums = lax.fori_loop(0, rows // 4, gather, tuple(jnp.zeros((8, lanes), F32) for _ in range(2 * ITERS)))
    spot = lax.broadcasted_iota(jnp.int32, (1, lanes), 1)
    line = jnp.zeros((1, lanes), F32)
    for k, part in enumerate(sums):
        whole = jnp.sum(jnp.sum(part, axis=0, keepdims=True), axis=1, keepdims=True)
        line = line + jnp.where(spot == k, whole, 0.0)
    lines[...] = jnp.broadcast_to(line, lines.shape)


def krylov(own, pieces):
    rows, cols, lanes = own.shape
    scratch = pltpu.VMEM((rows + 2 * REACH, cols + 2 * PAD, lanes), F32)
    vmem = pl.BlockSpec(memory_space=pltpu.VMEM)
    field = jax.ShapeDtypeStruct(own.shape, F32)
    return pl.pallas_call(
        krylov_body,
        out_shape=(field, field, jax.ShapeDtypeStruct((128, lanes), F32)),
        in_specs=[vmem] * (1 + len(pieces)),
        out_specs=(vmem, vmem, vmem),
        scratch_shapes=[scratch] * 4,
        compiler_params=pltpu.CompilerParams(vmem_limit_bytes=8 * 2**20),
        name="krylov",
    )(own, *pieces)


def weights_of(moments):
    unit = [m / moments[0] * 0.125**k for k, m in enumerate(moments)]

    def inner(a, b, shift):
        terms = [x * y * unit[i + j + shift] for i, x in enumerate(a) for j, y in enumerate(b)]
        return functools.reduce(lambda p, q: p + q, terms)

    residual, direction, answer = [1.0], [1.0], []
    norm = unit[0]
    for step in range(ITERS):
        alpha = norm / inner(direction, direction, 1)
        old = answer + [0.0] * (len(direction) - len(answer))
        answer = [a + alpha * d for a, d in zip(old, direction)]
        if step + 1 < ITERS:
            residual = [r - alpha * d for r, d in zip(residual + [0.0], [0.0] + direction)]
            fresh = inner(residual, residual, 0)
            ratio = fresh / norm
            direction = [r + ratio * d for r, d in zip(residual, direction + [0.0])]
            norm = fresh
    return [a * 0.125 ** (k + 1) for k, a in enumerate(answer)]


def combine_body(lines, own, first, second, out):
    line = jnp.sum(lines[...], axis=0, keepdims=True)
    spot = lax.broadcasted_iota(jnp.int32, line.shape, 1)
    moments = [jnp.sum(jnp.where(spot == k, line, 0.0), axis=1, keepdims=True) for k in range(2 * ITERS)]
    factors = [jnp.broadcast_to(f, own.shape[1:]) for f in weights_of(moments)]
    for r in range(own.shape[0]):
        out[r] = factors[0] * own[r] + factors[1] * first[r] + factors[2] * second[r]


def combine(lines, own, first, second):
    vmem = pl.BlockSpec(memory_space=pltpu.VMEM)
    return pl.pallas_call(
        combine_body,
        out_shape=jax.ShapeDtypeStruct(own.shape, F32),
        in_specs=[vmem] * 4,
        out_specs=vmem,
        compiler_params=pltpu.CompilerParams(vmem_limit_bytes=8 * 2**20),
        name="combine",
    )(lines, own, first, second)


def local(orbitals, occupations):
    scale = 4.0 * math.pi / (orbitals.shape[0] * 16)
    source = own_density(orbitals, occupations, scale)
    first, second, lines = krylov(source, halo(source))
    lines = lax.all_to_all(lines[:, None], EVERY, split_axis=0, concat_axis=0, tiled=True)[:, 0]
    return combine(lines, source, first, second)


def solution(mesh):
    split = Mesh(mesh.devices.reshape(SIDE, SIDE, SIDE, 2), EVERY)
    in_specs = (P(BAND, None, SPACE, None), P(BAND))
    out_specs = P(BAND, SPACE, None)
    return jax.shard_map(local, mesh=split, in_specs=in_specs, out_specs=out_specs, check_vma=False)
```
